256 devices in a mesh: gx: 16 (over x, z_lo), gy: 16 (over z_hi, y, core).
Axes of the slice: x: 4, y: 4, z: 8 (z_hi: 2, z_lo: 4; z = z_hi * 4 + z_lo), core: 2. Of those that a mesh axis runs over, the one named last changes fastest.
Arguments:
- migrated: float32 [256, 256, 128], P('gx', 'gy'), may hold values from -18 to 18
- prior_sample: float32 [256, 256, 128], P('gx', 'gy'), may hold values from -6 to 6
- damping: float32 [256, 256, 128], P('gx', 'gy'), may hold values from 0.2 to 2
- psf_bank: float32 [32, 32, 32, 32], replicated, may hold values from 0.05 to 3
- psf_index: int32 [16, 16, 6], P('gx', 'gy'), may hold values from 0 to 31
- z_shift: int32 [16, 16], P('gx', 'gy'), may hold values from 0 to 15
Outputs:
- solution: float32 [256, 256, 128], P('gx', 'gy')
- residual: float32 [256, 256, 128], P('gx', 'gy')
The draws below stay inside these ranges and needn't reach their ends.
All inputs are finite; a program needn't handle non-finite values.
Results may differ from the reference program's by a relative error of at most 0.0001.
Values sent between devices are 32-bit elements; how exact they have to be, the bound alone decides.
No kernel may reach another device: no remote copies, remote signals or barrier semaphores. Data moves between devices by JAX's collectives and lax.ppermute only.
A program may use at most 192 MiB of HBM per device.

```python
import math
import jax
import jax.numpy as jnp
from jax import lax

PATCH = 32
STRIDE = 16
NPZ = 6
BANK = 32
ITERS = 1
NZ = 128
NX = 256
NY = 256


def draw_migrated(key, part):
    ramp_x = jnp.arange(NX, dtype=jnp.float32)[:, None, None] / NX
    ramp_y = jnp.arange(NY, dtype=jnp.float32)[None, :, None] / NY
    ramp = jnp.exp(jnp.log(3.0) * 0.5 * (ramp_x + ramp_y))
    base = jnp.clip(jax.random.normal(key, (NX, NY, NZ), jnp.float32), -6.0, 6.0)
    return (base * ramp).astype(jnp.float32)


def plant(result, own_key, least, top_value):
    spot = [jax.random.randint(jax.random.fold_in(own_key, axis), (), 0, length) for axis, length in enumerate(result.shape)]
    main_axis = result.shape.index(max(result.shape))
    next_to = spot[:main_axis] + [(spot[main_axis] + 1) % result.shape[main_axis]] + spot[main_axis + 1:]
    return result.at[tuple(spot)].set(least).at[tuple(next_to)].set(top_value)


def block_scale(stream_key, shape, pieces, least, largest):
    loudness = 1.0
    for dim, shards_of in pieces:
        steps = jax.random.uniform(jax.random.fold_in(jax.random.fold_in(stream_key, 6), dim), (shards_of,), jnp.float32, least / len(pieces), largest / len(pieces))
        loudness = loudness * jnp.repeat(jnp.exp(steps), shape[dim] // shards_of).reshape((-1,) + (1,) * (len(shape) - 1 - dim))
    return loudness


def centred(own_key, dims, deviation, reach, split=(), kind=jnp.bfloat16):
    array = jax.random.normal(own_key, dims, jnp.float32) * deviation
    if len(split) > 0:
        array = block_scale(own_key, dims, split, -0.22, 0.18) * array
    return jnp.clip(array, min=-reach, max=reach).astype(kind)


def setup_inputs(seed: int = 0) -> dict:
    arg_keys = jax.random.split(jax.random.key(seed), 7)
    return {
        "migrated": draw_migrated(jax.random.fold_in(arg_keys[6], 71), 0),
        "prior_sample": centred(arg_keys[1], (NX, NY, NZ), 1.0, 6.0, ((0, 16), (1, 16)), jnp.float32),
        "damping": jnp.clip(jnp.exp(math.log(2.0) - 2.3025851 * jax.random.uniform(arg_keys[2], (NX, NY, NZ), jnp.float32) ** block_scale(arg_keys[2], (NX, NY, NZ), ((0, 16), (1, 16)), -0.2, 0.2)), 0.2, 2.0),
        "psf_bank": jnp.clip(jnp.exp(jax.random.uniform(arg_keys[3], (BANK, PATCH, PATCH, PATCH), jnp.float32, math.log(0.05), math.log(3.0))), 0.05, 3.0),
        "psf_index": plant(jax.random.randint(arg_keys[4], (NX // STRIDE, NY // STRIDE, NPZ), 0, BANK), jax.random.fold_in(arg_keys[4], 1), 0, BANK - 1).astype(jnp.int32),
        "z_shift": plant(jax.random.randint(arg_keys[5], (NX // STRIDE, NY // STRIDE), 0, STRIDE), jax.random.fold_in(arg_keys[5], 1), 0, STRIDE - 1).astype(jnp.int32),
    }


def taper_of(size):
    return jnp.sin(math.pi * (jnp.arange(size, dtype=jnp.float32) + 0.5) / size)


def hessian(field, psf_bank, psf_index, z_shift):
    half = PATCH // 2
    span = half * (NPZ + 1)
    cols_y = NY // half
    rows_x = NX // half
    win = taper_of(PATCH)
    cube = win[:, None, None] * win[None, :, None] * win[None, None, :]
    padded = jnp.pad(field, ((0, half), (0, half), (0, 0)))

    def cut_column(column, shift):
        return lax.dynamic_slice_in_dim(column, shift, span, 2)

    def put_column(piece, shift):
        return lax.dynamic_update_slice_in_dim(jnp.zeros((PATCH, PATCH, NZ), piece.dtype), piece, shift, 2)

    def add_row(total, row):
        slab = lax.dynamic_slice_in_dim(padded, row * half, PATCH, 0)
        tiles = slab.reshape(PATCH, cols_y + 1, half, NZ)
        columns = jnp.concatenate([tiles[:, :-1], tiles[:, 1:]], axis=2)
        shifts = lax.dynamic_index_in_dim(z_shift, row, 0, keepdims=False)
        cut = jax.vmap(cut_column, in_axes=(1, 0))(columns, shifts)
        ztiles = cut.reshape(cols_y, PATCH, PATCH, NPZ + 1, half)
        blocks = jnp.concatenate([ztiles[..., :-1, :], ztiles[..., 1:, :]], axis=-1)
        blocks = jnp.moveaxis(blocks, 3, 1) * cube
        chosen = psf_bank[lax.dynamic_index_in_dim(psf_index, row, 0, keepdims=False)]
        spectrum = jnp.fft.fftn(blocks, axes=(2, 3, 4))
        image = jnp.real(jnp.fft.ifftn(spectrum * chosen, axes=(2, 3, 4))) * cube
        image = jnp.moveaxis(image, 1, 3)
        zsum = jnp.zeros((cols_y, PATCH, PATCH, NPZ + 1, half), image.dtype)
        zsum = zsum.at[..., :-1, :].add(image[..., :half]).at[..., 1:, :].add(image[..., half:])
        placed = jax.vmap(put_column)(zsum.reshape(cols_y, PATCH, PATCH, span), shifts)
        placed = jnp.moveaxis(placed, 0, 1)
        ysum = jnp.zeros((PATCH, cols_y + 1, half, NZ), placed.dtype)
        ysum = ysum.at[:, :-1].add(placed[:, :, :half]).at[:, 1:].add(placed[:, :, half:])
        contribution = ysum.reshape(PATCH, NY + half, NZ)
        current = lax.dynamic_slice_in_dim(total, row * half, PATCH, 0)
        return lax.dynamic_update_slice_in_dim(total, current + contribution, row * half, 0), None

    total, _ = lax.scan(add_row, jnp.zeros_like(padded), jnp.arange(rows_x, dtype=jnp.int32))
    return total[:NX, :NY]


def reference(migrated, prior_sample, damping, psf_bank, psf_index, z_shift):
    right_side = migrated + damping * prior_sample
    solution = jnp.zeros_like(right_side)
    residual = right_side
    direction = right_side
    norm_now = jnp.sum(residual * residual)
    for step in range(ITERS):
        image = hessian(direction, psf_bank, psf_index, z_shift) + damping * direction
        alpha = norm_now / jnp.sum(direction * image)
        solution = solution + alpha * direction
        residual = residual - alpha * image
        norm_next = jnp.sum(residual * residual)
        direction = residual + (norm_next / norm_now) * direction
        norm_now = norm_next
    return solution, residual
```

```python
import math

import numpy as np
import jax
import jax.numpy as jnp
from jax import lax
from jax.experimental import pallas as pl
from jax.experimental.pallas import tpu as pltpu
from jax.sharding import PartitionSpec as P

PATCH = 32
HALF = 16
NPZ = 6
KZ = 17
LANES = 128
SUB = 8
VMEM = pltpu.VMEM


def z_table():
    table = np.zeros((160, 2 * LANES))
    taper = np.sin(math.pi * (np.arange(PATCH) + 0.5) / PATCH)
    for p in range(NPZ):
        for cell in range(PATCH):
            for kz in range(KZ):
                phase = 2.0 * math.pi * (kz * cell % PATCH) / PATCH
                row = 16 + 16 * p + cell
                table[row, KZ * p + kz] = taper[cell] * math.cos(phase)
                if 0 < kz < HALF:
                    table[row, LANES + KZ * p + kz] = -taper[cell] * math.sin(phase)
    return table.astype(np.float32)


def pick_table():
    table = np.zeros((NPZ, PATCH, 2 * LANES))
    for p in range(NPZ):
        for kz in range(KZ):
            table[p, kz, KZ * p + kz] = 1.0
            if 0 < kz < HALF:
                table[p, PATCH - kz, LANES + KZ * p + kz] = 1.0
    return table.astype(np.float32)


TAPER = [math.sin(math.pi * (i + 0.5) / PATCH) for i in range(PATCH)]


def twiddle(value, k, n, sign):
    k %= n
    re, im = value
    if k == 0:
        return value
    if 4 * k == n:
        return (-im, re) if sign > 0 else (im, -re)
    if 2 * k == n:
        return (-re, -im)
    if 4 * k == 3 * n:
        return (im, -re) if sign > 0 else (-im, re)
    c = math.cos(2.0 * math.pi * k / n)
    s = sign * math.sin(2.0 * math.pi * k / n)
    if 8 * k % n == 0:
        h = abs(c)
        cs, ss = (1 if c > 0 else -1), (1 if s > 0 else -1)
        if cs == ss:
            a, b = re - im, re + im
            return (a * (h * cs), b * (h * cs))
        a, b = re + im, im - re
        return (a * (h * cs), b * (h * cs))
    return (re * c - im * s, re * s + im * c)


def add(a, b):
    return (a[0] + b[0], a[1] + b[1])


def sub(a, b):
    return (a[0] - b[0], a[1] - b[1])


def dft4(x, sign):
    a, b = add(x[0], x[2]), sub(x[0], x[2])
    c, d = add(x[1], x[3]), twiddle(sub(x[1], x[3]), 1, 4, sign)
    return [add(a, c), add(b, d), sub(a, c), sub(b, d)]


def dft8(x, sign):
    even = dft4(x[0::2], sign)
    odd = [twiddle(v, k, 8, sign) for k, v in enumerate(dft4(x[1::2], sign))]
    return [add(even[k], odd[k]) for k in range(4)] + [sub(even[k], odd[k]) for k in range(4)]


def dft32(load, sign):
    first = []
    for n2 in range(8):
        part = dft4([load(8 * n1 + n2) for n1 in range(4)], sign)
        first.append([twiddle(v, n2 * k1, 32, sign) for k1, v in enumerate(part)])
    out = [None] * 32
    for k1 in range(4):
        part = dft8([first[n2][k1] for n2 in range(8)], sign)
        for k2 in range(8):
            out[k1 + 4 * k2] = part[k2]
    return out


def halves(value):
    high = value.astype(jnp.bfloat16)
    return high, (value - high.astype(jnp.float32)).astype(jnp.bfloat16)


def dot(a, b, contract_b):
    return lax.dot_general(a, b, (((1,), (contract_b,)), ((), ())), preferred_element_type=jnp.float32)


def dot3(a, b, contract_b):
    return dot(a[0], b[0], contract_b) + (dot(a[1], b[0], contract_b) + dot(a[0], b[1], contract_b))


def spectra_kernel(index_ref, bank_ref, pick_ref, out_ref, cubes, back, sems):
    copies = [
        pltpu.make_async_copy(bank_ref.at[index_ref[p]], cubes.at[p], sems.at[p]) for p in range(NPZ)
    ]
    for copy in copies:
        copy.start()
    total = None
    for p, copy in enumerate(copies):
        copy.wait()
        high, low = halves(cubes[p].reshape(PATCH * PATCH, PATCH))
        pick = pick_ref[p].astype(jnp.bfloat16)
        part = dot(high, pick, 0) + dot(low, pick, 0)
        total = part if total is None else total + part
    out_ref[...] = total[:, :LANES]
    back[...] = total[:, LANES:]
    row = lax.broadcasted_iota(jnp.int32, (SUB, LANES), 0)
    mirror = (SUB - row) % SUB
    for kx in range(PATCH):
        source = (PATCH - kx) % PATCH
        turned = [
            jnp.take_along_axis(back[pl.ds(source * PATCH + SUB * g, SUB), :], mirror, axis=0, mode="promise_in_bounds") for g in range(4)
        ]
        for g in range(4):
            rows = pl.ds(kx * PATCH + SUB * g, SUB)
            mirrored = jnp.where(row == 0, turned[(4 - g) % 4], turned[3 - g])
            out_ref[rows, :] = out_ref[rows, :] + mirrored


def spectra_of(index, bank):
    return pl.pallas_call(
        spectra_kernel,
        out_shape=jax.ShapeDtypeStruct((PATCH * PATCH, LANES), jnp.float32),
        in_specs=[
            pl.BlockSpec(memory_space=pltpu.SMEM),
            pl.BlockSpec(memory_space=pltpu.HBM),
            pl.BlockSpec(memory_space=VMEM),
        ],
        out_specs=pl.BlockSpec(memory_space=VMEM),
        scratch_shapes=[
            VMEM((NPZ, PATCH, PATCH, PATCH), jnp.float32),
            VMEM((PATCH * PATCH, LANES), jnp.float32),
            pltpu.SemaphoreType.DMA((NPZ,)),
        ],
        compiler_params=pltpu.CompilerParams(vmem_limit_bytes=50 * 2**20),
        cost_estimate=pl.CostEstimate(flops=400_000_000, bytes_accessed=8_000_000, transcendentals=0),
        name="spectra",
    )(index, bank, pick_table())


def patches_kernel(shift_ref, table_ref, spectra_ref, damping_ref, b00, b10, b01, b11,
                   o00, o10, o01, o11, sums_ref, real, imag):
    window = halves(pltpu.roll(table_ref[...], shift_ref[0] + 144, 0)[:LANES])
    for xq, yq, block in ((0, 0, b00), (1, 0, b10), (0, 1, b01), (1, 1, b11)):
        result = dot3(halves(block[...].reshape(HALF * HALF, LANES)), window, 0)
        for i in range(HALF):
            rows = pl.ds((HALF * xq + i) * PATCH + HALF * yq, HALF)
            real[rows, :] = result[HALF * i : HALF * (i + 1), :LANES]
            imag[rows, :] = result[HALF * i : HALF * (i + 1), LANES:]

    def strided(h, y):
        return pl.ds(SUB * PATCH * h + y, SUB, stride=PATCH)

    for h in range(4):
        out = dft32(lambda y: (real[strided(h, y), :] * TAPER[y], imag[strided(h, y), :] * TAPER[y]), -1)
        for k, (re, im) in enumerate(out):
            real[strided(h, k), :] = re
            imag[strided(h, k), :] = im

    energy = jnp.zeros((SUB, LANES), jnp.float32)
    for g in range(4):
        def rows(x):
            return pl.ds(x * PATCH + SUB * g, SUB)

        out = dft32(lambda x: (real[rows(x), :] * TAPER[x], imag[rows(x), :] * TAPER[x]), -1)
        scaled = []
        for k, (re, im) in enumerate(out):
            s = spectra_ref[rows(k), :]
            sre, sim = s * re, s * im
            energy = energy + (sre * re + sim * im)
            scaled.append((sre, sim))
        out = dft32(lambda k: scaled[k], 1)
        for x, (re, im) in enumerate(out):
            real[rows(x), :] = re * (TAPER[x] / PATCH**3)
            imag[rows(x), :] = im * (TAPER[x] / PATCH**3)

    field = b00[...]
    square = field * field
    rr = jnp.sum(square)
    dd = jnp.sum(square * damping_ref[...]) + jnp.sum(energy) * (1.0 / PATCH**3)
    lane = lax.broadcasted_iota(jnp.int32, sums_ref.shape, len(sums_ref.shape) - 1)
    sums_ref[...] = jnp.where(lane == 0, rr, jnp.where(lane == 1, dd, 0.0))

    for h in range(4):
        out = dft32(lambda k: (real[strided(h, k), :], imag[strided(h, k), :]), 1)
        for y, (re, im) in enumerate(out):
            real[strided(h, y), :] = re * TAPER[y]
            imag[strided(h, y), :] = im * TAPER[y]

    for xq in range(2):
        rows = pl.ds(xq * 512, 512)
        both = jnp.concatenate([real[rows, :], imag[rows, :]], axis=1)
        result = dot3(halves(both), window, 1).reshape(HALF, PATCH, LANES)
        near, far = ((o00, o01), (o10, o11))[xq]
        near[...] = result[:, :HALF]
        far[...] = result[:, HALF:]


def patches(shift, spectra, damping, blocks):
    block = jax.ShapeDtypeStruct(blocks[0].shape, jnp.float32)
    vmem = pl.BlockSpec(memory_space=VMEM)
    return pl.pallas_call(
        patches_kernel,
        out_shape=[block] * 4 + [jax.ShapeDtypeStruct((256, 1, LANES), jnp.float32)],
        in_specs=[pl.BlockSpec(memory_space=pltpu.SMEM)] + [vmem] * 7,
        out_specs=[vmem] * 5,
        scratch_shapes=[VMEM((PATCH * PATCH, LANES), jnp.float32)] * 2,
        compiler_params=pltpu.CompilerParams(vmem_limit_bytes=32 * 2**20),
        cost_estimate=pl.CostEstimate(flops=800_000_000, bytes_accessed=4_000_000, transcendentals=0),
        name="patches",
    )(shift, z_table(), spectra, damping, *blocks)


def finish_kernel(sums_ref, rhs_ref, damping_ref, own, r10, r01, r11, solution_ref, residual_ref):
    totals = jnp.sum(sums_ref[...], axis=(0, 1), keepdims=True)[0]
    lane = lax.broadcasted_iota(jnp.int32, totals.shape, 1)
    rr = jnp.sum(jnp.where(lane == 0, totals, 0.0), axis=1, keepdims=True)
    dd = jnp.sum(jnp.where(lane == 1, totals, 0.0), axis=1, keepdims=True)
    alpha = (rr / dd)[None]
    rhs = rhs_ref[...]
    image = ((own[...] + r10[...]) + (r01[...] + r11[...])) + damping_ref[...] * rhs
    solution_ref[...] = alpha * rhs
    residual_ref[...] = rhs - alpha * image


def finish(sums, rhs, damping, parts):
    block = jax.ShapeDtypeStruct(rhs.shape, jnp.float32)
    vmem = pl.BlockSpec(memory_space=VMEM)
    return pl.pallas_call(
        finish_kernel,
        out_shape=[block, block],
        in_specs=[vmem] * 7,
        out_specs=[vmem] * 2,
        compiler_params=pltpu.CompilerParams(vmem_limit_bytes=8 * 2**20),
        cost_estimate=pl.CostEstimate(flops=1_000_000, bytes_accessed=1_000_000, transcendentals=0),
        name="finish",
    )(sums, rhs, damping, *parts)


def moved(x, by_x, by_y):
    nx, ny = lax.axis_size("gx"), lax.axis_size("gy")
    pairs = [
        (i * ny + j, (i + by_x) * ny + j + by_y)
        for i in range(nx)
        for j in range(ny)
        if 0 <= i + by_x < nx and 0 <= j + by_y < ny
    ]
    return lax.ppermute(x, ("gx", "gy"), pairs)


def body(migrated, prior_sample, damping, psf_bank, psf_index, z_shift):
    rhs = migrated + damping * prior_sample
    halo = [moved(rhs, -1, 0), moved(rhs, 0, -1), moved(rhs, -1, -1)]
    spectra = spectra_of(psf_index.reshape(NPZ), psf_bank)
    own, o10, o01, o11, sums = patches(z_shift.reshape(1), spectra, damping, [rhs] + halo)
    sums = lax.all_to_all(sums, ("gx", "gy"), 0, 0)
    back = [moved(o10, 1, 0), moved(o01, 0, 1), moved(o11, 1, 1)]
    return tuple(finish(sums, rhs, damping, [own] + back))


def solution(mesh):
    block = P("gx", "gy", None)
    return jax.shard_map(
        body,
        mesh=mesh,
        in_specs=(block, block, block, P(), block, P("gx", "gy")),
        out_specs=(block, block),
        check_vma=False,
    )
```

```python
import math

import numpy as np
import jax
import jax.numpy as jnp
from jax import lax
from jax.experimental import pallas as pl
from jax.experimental.pallas import tpu as pltpu
from jax.sharding import PartitionSpec as P

PATCH = 32
HALF = 16
NPZ = 6
KZ = 17
LANES = 128
SUB = 8
VMEM = pltpu.VMEM


def z_table():
    table = np.zeros((160, 2 * LANES))
    taper = np.sin(math.pi * (np.arange(PATCH) + 0.5) / PATCH)
    for p in range(NPZ):
        for cell in range(PATCH):
            for kz in range(KZ):
                phase = 2.0 * math.pi * (kz * cell % PATCH) / PATCH
                row = 16 + 16 * p + cell
                table[row, KZ * p + kz] = taper[cell] * math.cos(phase)
                if 0 < kz < HALF:
                    table[row, LANES + KZ * p + kz] = -taper[cell] * math.sin(phase)
    return table.astype(np.float32)


TAPER = [math.sin(math.pi * (i + 0.5) / PATCH) for i in range(PATCH)]


def twiddle(value, k, n, sign):
    k %= n
    re, im = value
    if k == 0:
        return value
    if 4 * k == n:
        return (-im, re) if sign > 0 else (im, -re)
    if 2 * k == n:
        return (-re, -im)
    if 4 * k == 3 * n:
        return (im, -re) if sign > 0 else (-im, re)
    c = math.cos(2.0 * math.pi * k / n)
    s = sign * math.sin(2.0 * math.pi * k / n)
    if 8 * k % n == 0:
        h = abs(c)
        cs, ss = (1 if c > 0 else -1), (1 if s > 0 else -1)
        if cs == ss:
            a, b = re - im, re + im
            return (a * (h * cs), b * (h * cs))
        a, b = re + im, im - re
        return (a * (h * cs), b * (h * cs))
    return (re * c - im * s, re * s + im * c)


def add(a, b):
    return (a[0] + b[0], a[1] + b[1])


def sub(a, b):
    return (a[0] - b[0], a[1] - b[1])


def dft4(x, sign):
    a, b = add(x[0], x[2]), sub(x[0], x[2])
    c, d = add(x[1], x[3]), twiddle(sub(x[1], x[3]), 1, 4, sign)
    return [add(a, c), add(b, d), sub(a, c), sub(b, d)]


def dft8(x, sign):
    even = dft4(x[0::2], sign)
    odd = [twiddle(v, k, 8, sign) for k, v in enumerate(dft4(x[1::2], sign))]
    return [add(even[k], odd[k]) for k in range(4)] + [sub(even[k], odd[k]) for k in range(4)]


def dft32(load, sign):
    first = []
    for n2 in range(8):
        part = dft4([load(8 * n1 + n2) for n1 in range(4)], sign)
        first.append([twiddle(v, n2 * k1, 32, sign) for k1, v in enumerate(part)])
    out = [None] * 32
    for k1 in range(4):
        part = dft8([first[n2][k1] for n2 in range(8)], sign)
        for k2 in range(8):
            out[k1 + 4 * k2] = part[k2]
    return out


def halves(value):
    high = value.astype(jnp.bfloat16)
    return high, (value - high.astype(jnp.float32)).astype(jnp.bfloat16)


def dot(a, b, contract_b):
    return lax.dot_general(a, b, (((1,), (contract_b,)), ((), ())), preferred_element_type=jnp.float32)


def dot3(a, b, contract_b):
    return dot(a[0], b[0], contract_b) + (dot(a[1], b[0], contract_b) + dot(a[0], b[1], contract_b))


def prepare_kernel(index_ref, shift_ref, bank_ref, table_ref, block_ref,
                   spectra_ref, window_ref, own_ref, cubes, back, sems):
    copies = [
        pltpu.make_async_copy(bank_ref.at[index_ref[p]], cubes.at[p], sems.at[p]) for p in range(NPZ)
    ]
    for copy in copies:
        copy.start()

    window = pltpu.roll(table_ref[...], shift_ref[0] + 144, 0)[:LANES]
    window_ref[...] = window
    own_ref[...] = dot3(halves(block_ref[...].reshape(HALF * HALF, LANES)), halves(window), 0)

    source = lax.broadcasted_iota(jnp.int32, (NPZ * PATCH, 2 * LANES), 0)
    lane = lax.broadcasted_iota(jnp.int32, (NPZ * PATCH, 2 * LANES), 1)
    p, kz = source // PATCH, source % PATCH
    target = jnp.where(kz < KZ, KZ * p + kz, LANES + KZ * p + PATCH - kz)
    pick = jnp.where(lane == target, 1.0, 0.0).astype(jnp.bfloat16)

    for copy in copies:
        copy.wait()
    total = None
    for first, last in ((0, 4), (4, NPZ)):
        joined = jnp.concatenate(
            [cubes[q].reshape(PATCH * PATCH, PATCH) for q in range(first, last)], axis=1
        )
        high, low = halves(joined)
        rows = pick[PATCH * first : PATCH * last]
        part = dot(high, rows, 0) + dot(low, rows, 0)
        total = part if total is None else total + part
    spectra_ref[...] = total[:, :LANES]
    back[...] = total[:, LANES:]
    row = lax.broadcasted_iota(jnp.int32, (SUB, LANES), 0)
    mirror = (SUB - row) % SUB
    for kx in range(PATCH):
        other = (PATCH - kx) % PATCH
        turned = [
            jnp.take_along_axis(
                back[pl.ds(other * PATCH + SUB * g, SUB), :], mirror, axis=0, mode="promise_in_bounds"
            )
            for g in range(4)
        ]
        for g in range(4):
            rows = pl.ds(kx * PATCH + SUB * g, SUB)
            mirrored = jnp.where(row == 0, turned[(4 - g) % 4], turned[3 - g])
            spectra_ref[rows, :] = spectra_ref[rows, :] + mirrored


def prepare(index, shift, bank, rhs):
    smem = pl.BlockSpec(memory_space=pltpu.SMEM)
    vmem = pl.BlockSpec(memory_space=VMEM)
    return pl.pallas_call(
        prepare_kernel,
        out_shape=[
            jax.ShapeDtypeStruct((PATCH * PATCH, LANES), jnp.float32),
            jax.ShapeDtypeStruct((LANES, 2 * LANES), jnp.float32),
            jax.ShapeDtypeStruct((HALF * HALF, 2 * LANES), jnp.float32),
        ],
        in_specs=[smem, smem, pl.BlockSpec(memory_space=pltpu.HBM), vmem, vmem],
        out_specs=[vmem] * 3,
        scratch_shapes=[
            VMEM((NPZ, PATCH, PATCH, PATCH), jnp.float32),
            VMEM((PATCH * PATCH, LANES), jnp.float32),
            pltpu.SemaphoreType.DMA((NPZ,)),
        ],
        compiler_params=pltpu.CompilerParams(vmem_limit_bytes=50 * 2**20),
        cost_estimate=pl.CostEstimate(flops=400_000_000, bytes_accessed=8_000_000, transcendentals=0),
        name="prepare",
    )(index, shift, bank, z_table(), rhs)


PITCH = 40


def patches_kernel(window_ref, spectra_ref, own_ref, b10, b01, b11,
                   o10, o01, o11, near_ref, energy_ref, real, imag):
    window = halves(window_ref[...])

    for xq, yq, block in ((0, 0, None), (1, 0, b10), (0, 1, b01), (1, 1, b11)):
        if block is None:
            result = own_ref[...]
        else:
            result = dot3(halves(block[...].reshape(HALF * HALF, LANES)), window, 0)
        for i in range(HALF):
            rows = pl.ds((HALF * xq + i) * PITCH + HALF * yq, HALF)
            real[rows, :] = result[HALF * i : HALF * (i + 1), :LANES]
            imag[rows, :] = result[HALF * i : HALF * (i + 1), LANES:]

    def strided(h, y):
        return pl.ds(SUB * PITCH * h + y, SUB, stride=PITCH)

    for h in range(4):
        out = dft32(lambda y: (real[strided(h, y), :] * TAPER[y], imag[strided(h, y), :] * TAPER[y]), -1)
        for k, (re, im) in enumerate(out):
            real[strided(h, k), :] = re
            imag[strided(h, k), :] = im

    energy = jnp.zeros((SUB, LANES), jnp.float32)
    for g in range(4):
        def rows(x):
            return pl.ds(x * PITCH + SUB * g, SUB)

        out = dft32(lambda x: (real[rows(x), :] * TAPER[x], imag[rows(x), :] * TAPER[x]), -1)
        scaled = []
        for k, (re, im) in enumerate(out):
            s = spectra_ref[pl.ds(k * PATCH + SUB * g, SUB), :]
            sre, sim = s * re, s * im
            energy = energy + (sre * re + sim * im)
            scaled.append((sre, sim))
        out = dft32(lambda k: scaled[k], 1)
        for x, (re, im) in enumerate(out):
            real[rows(x), :] = re * (TAPER[x] / PATCH**3)
            imag[rows(x), :] = im * (TAPER[x] / PATCH**3)
    energy_ref[...] = energy

    for h in range(4):
        out = dft32(lambda k: (real[strided(h, k), :], imag[strided(h, k), :]), 1)
        for y, (re, im) in enumerate(out):
            real[strided(h, y), :] = re * TAPER[y]
            imag[strided(h, y), :] = im * TAPER[y]

    for xq, yq, out in ((0, 0, near_ref), (1, 1, o11), (0, 1, o01), (1, 0, o10)):
        pieces = []
        for i in range(HALF):
            rows = pl.ds((HALF * xq + i) * PITCH + HALF * yq, HALF)
            pieces.append(jnp.concatenate([real[rows, :], imag[rows, :]], axis=1))
        both = jnp.concatenate(pieces, axis=0)
        if out is near_ref:
            near_ref[...] = both
        else:
            out[...] = dot3(halves(both), window, 1).reshape(HALF, HALF, LANES)


def patches(window, spectra, own, blocks):
    block = jax.ShapeDtypeStruct(blocks[0].shape, jnp.float32)
    vmem = pl.BlockSpec(memory_space=VMEM)
    return pl.pallas_call(
        patches_kernel,
        out_shape=[block] * 3
        + [jax.ShapeDtypeStruct(own.shape, jnp.float32), jax.ShapeDtypeStruct((SUB, LANES), jnp.float32)],
        in_specs=[vmem] * 6,
        out_specs=[vmem] * 5,
        scratch_shapes=[VMEM((PATCH * PITCH, LANES), jnp.float32)] * 2,
        compiler_params=pltpu.CompilerParams(vmem_limit_bytes=32 * 2**20),
        cost_estimate=pl.CostEstimate(flops=800_000_000, bytes_accessed=4_000_000, transcendentals=0),
        name="patches",
    )(window, spectra, own, *blocks)


def near_kernel(window_ref, near_ref, energy_ref, rhs_ref, damping_ref, image_ref, sums_ref):
    field = rhs_ref[...]
    square = field * field
    damped = damping_ref[...]
    rr = jnp.sum(square)
    dd = jnp.sum(square * damped) + jnp.sum(energy_ref[...]) * (1.0 / PATCH**3)
    lane = lax.broadcasted_iota(jnp.int32, sums_ref.shape, len(sums_ref.shape) - 1)
    sums_ref[...] = jnp.where(lane == 0, rr, jnp.where(lane == 1, dd, 0.0))
    own = dot3(halves(near_ref[...]), halves(window_ref[...]), 1)
    image_ref[...] = own.reshape(field.shape) + damped * field


def near(window, inner, energy, rhs, damping):
    vmem = pl.BlockSpec(memory_space=VMEM)
    return pl.pallas_call(
        near_kernel,
        out_shape=[
            jax.ShapeDtypeStruct(rhs.shape, jnp.float32),
            jax.ShapeDtypeStruct((256, 1, 2), jnp.float32),
        ],
        in_specs=[vmem] * 5,
        out_specs=[vmem] * 2,
        compiler_params=pltpu.CompilerParams(vmem_limit_bytes=32 * 2**20),
        cost_estimate=pl.CostEstimate(flops=20_000_000_000, bytes_accessed=40_000_000, transcendentals=0),
        name="near",
    )(window, inner, energy, rhs, damping)


def finish_kernel(sums_ref, rhs_ref, own, r10, r01, r11, solution_ref, residual_ref):
    totals = jnp.sum(sums_ref[...], axis=(0, 1), keepdims=True)[0]
    lane = lax.broadcasted_iota(jnp.int32, totals.shape, 1)
    rr = jnp.sum(jnp.where(lane == 0, totals, 0.0), axis=1, keepdims=True)
    dd = jnp.sum(jnp.where(lane == 1, totals, 0.0), axis=1, keepdims=True)
    alpha = (rr / dd)[None]
    rhs = rhs_ref[...]
    image = (own[...] + r10[...]) + (r01[...] + r11[...])
    solution_ref[...] = alpha * rhs
    residual_ref[...] = rhs - alpha * image


def finish(sums, rhs, parts):
    block = jax.ShapeDtypeStruct(rhs.shape, jnp.float32)
    vmem = pl.BlockSpec(memory_space=VMEM)
    return pl.pallas_call(
        finish_kernel,
        out_shape=[block, block],
        in_specs=[vmem] * 6,
        out_specs=[vmem] * 2,
        compiler_params=pltpu.CompilerParams(vmem_limit_bytes=8 * 2**20),
        cost_estimate=pl.CostEstimate(flops=1_000_000, bytes_accessed=1_000_000, transcendentals=0),
        name="finish",
    )(sums, rhs, *parts)


def moved(x, by_x, by_y):
    nx, ny = lax.axis_size("gx"), lax.axis_size("gy")
    pairs = [
        (i * ny + j, (i + by_x) * ny + j + by_y)
        for i in range(nx)
        for j in range(ny)
        if 0 <= i + by_x < nx and 0 <= j + by_y < ny
    ]
    return lax.ppermute(x, ("gx", "gy"), pairs)


def body(migrated, prior_sample, damping, psf_bank, psf_index, z_shift):
    rhs = migrated + damping * prior_sample
    halo = [moved(rhs, -1, 0), moved(rhs, 0, -1), moved(rhs, -1, -1)]
    spectra, window, own = prepare(psf_index.reshape(NPZ), z_shift.reshape(1), psf_bank, rhs)
    o10, o01, o11, inner, energy = patches(window, spectra, own, halo)
    back = [moved(o10, 1, 0), moved(o01, 0, 1), moved(o11, 1, 1)]
    image, sums = near(window, inner, energy, rhs, damping)
    sums = lax.all_to_all(sums, ("gx", "gy"), 0, 0)
    return tuple(finish(sums, rhs, [image] + back))


def solution(mesh):
    block = P("gx", "gy", None)
    return jax.shard_map(
        body,
        mesh=mesh,
        in_specs=(block, block, block, P(), block, P("gx", "gy")),
        out_specs=(block, block),
        check_vma=False,
    )
```

```python
import math

import numpy as np
import jax
import jax.numpy as jnp
from jax import lax
from jax.experimental import pallas as pl
from jax.experimental.pallas import tpu as pltpu
from jax.sharding import PartitionSpec as P

PATCH = 32
HALF = 16
NPZ = 6
KZ = 17
LANES = 128
SUB = 8
VMEM = pltpu.VMEM


def z_table():
    table = np.zeros((160, 2 * LANES))
    taper = np.sin(math.pi * (np.arange(PATCH) + 0.5) / PATCH)
    for p in range(NPZ):
        for cell in range(PATCH):
            for kz in range(KZ):
                phase = 2.0 * math.pi * (kz * cell % PATCH) / PATCH
                row = 16 + 16 * p + cell
                table[row, KZ * p + kz] = taper[cell] * math.cos(phase)
                if 0 < kz < HALF:
                    table[row, LANES + KZ * p + kz] = -taper[cell] * math.sin(phase)
    return table.astype(np.float32)


TAPER = [math.sin(math.pi * (i + 0.5) / PATCH) for i in range(PATCH)]


def twiddle(value, k, n, sign):
    k %= n
    re, im = value
    if k == 0:
        return value
    if 4 * k == n:
        return (-im, re) if sign > 0 else (im, -re)
    if 2 * k == n:
        return (-re, -im)
    if 4 * k == 3 * n:
        return (im, -re) if sign > 0 else (-im, re)
    c = math.cos(2.0 * math.pi * k / n)
    s = sign * math.sin(2.0 * math.pi * k / n)
    if 8 * k % n == 0:
        h = abs(c)
        cs, ss = (1 if c > 0 else -1), (1 if s > 0 else -1)
        if cs == ss:
            a, b = re - im, re + im
            return (a * (h * cs), b * (h * cs))
        a, b = re + im, im - re
        return (a * (h * cs), b * (h * cs))
    return (re * c - im * s, re * s + im * c)


def add(a, b):
    return (a[0] + b[0], a[1] + b[1])


def sub(a, b):
    return (a[0] - b[0], a[1] - b[1])


def dft4(x, sign):
    a, b = add(x[0], x[2]), sub(x[0], x[2])
    c, d = add(x[1], x[3]), twiddle(sub(x[1], x[3]), 1, 4, sign)
    return [add(a, c), add(b, d), sub(a, c), sub(b, d)]


def dft8(x, sign):
    even = dft4(x[0::2], sign)
    odd = [twiddle(v, k, 8, sign) for k, v in enumerate(dft4(x[1::2], sign))]
    return [add(even[k], odd[k]) for k in range(4)] + [sub(even[k], odd[k]) for k in range(4)]


def dft32(load, sign):
    first = []
    for n2 in range(8):
        part = dft4([load(8 * n1 + n2) for n1 in range(4)], sign)
        first.append([twiddle(v, n2 * k1, 32, sign) for k1, v in enumerate(part)])
    out = [None] * 32
    for k1 in range(4):
        part = dft8([first[n2][k1] for n2 in range(8)], sign)
        for k2 in range(8):
            out[k1 + 4 * k2] = part[k2]
    return out


def halves(value):
    high = value.astype(jnp.bfloat16)
    return high, (value - high.astype(jnp.float32)).astype(jnp.bfloat16)


def dot(a, b, contract_b):
    return lax.dot_general(a, b, (((1,), (contract_b,)), ((), ())), preferred_element_type=jnp.float32)


def dot3(a, b, contract_b):
    return dot(a[0], b[0], contract_b) + (dot(a[1], b[0], contract_b) + dot(a[0], b[1], contract_b))


def prepare_kernel(index_ref, shift_ref, bank_ref, table_ref, block_ref,
                   spectra_ref, window_ref, own_ref, cubes, back, sems):
    copies = [
        pltpu.make_async_copy(bank_ref.at[index_ref[p]], cubes.at[p], sems.at[p]) for p in range(NPZ)
    ]
    for copy in copies:
        copy.start()

    window = pltpu.roll(table_ref[...], shift_ref[0] + 144, 0)[:LANES]
    window_ref[...] = window
    own_ref[...] = dot3(halves(block_ref[...].reshape(HALF * HALF, LANES)), halves(window), 0)

    source = lax.broadcasted_iota(jnp.int32, (NPZ * PATCH, 2 * LANES), 0)
    lane = lax.broadcasted_iota(jnp.int32, (NPZ * PATCH, 2 * LANES), 1)
    p, kz = source // PATCH, source % PATCH
    target = jnp.where(kz < KZ, KZ * p + kz, LANES + KZ * p + PATCH - kz)
    pick = jnp.where(lane == target, 1.0, 0.0).astype(jnp.bfloat16)

    for copy in copies:
        copy.wait()
    total = None
    for first, last in ((0, 4), (4, NPZ)):
        joined = jnp.concatenate(
            [cubes[q].reshape(PATCH * PATCH, PATCH) for q in range(first, last)], axis=1
        )
        high, low = halves(joined)
        rows = pick[PATCH * first : PATCH * last]
        part = dot(high, rows, 0) + dot(low, rows, 0)
        total = part if total is None else total + part
    spectra_ref[...] = total[:, :LANES]
    back[...] = total[:, LANES:]
    row = lax.broadcasted_iota(jnp.int32, (SUB, LANES), 0)
    mirror = (SUB - row) % SUB
    for kx in range(PATCH):
        other = (PATCH - kx) % PATCH
        turned = [
            jnp.take_along_axis(
                back[pl.ds(other * PATCH + SUB * g, SUB), :], mirror, axis=0, mode="promise_in_bounds"
            )
            for g in range(4)
        ]
        for g in range(4):
            rows = pl.ds(kx * PATCH + SUB * g, SUB)
            mirrored = jnp.where(row == 0, turned[(4 - g) % 4], turned[3 - g])
            spectra_ref[rows, :] = spectra_ref[rows, :] + mirrored


def prepare(index, shift, bank, rhs):
    smem = pl.BlockSpec(memory_space=pltpu.SMEM)
    vmem = pl.BlockSpec(memory_space=VMEM)
    return pl.pallas_call(
        prepare_kernel,
        out_shape=[
            jax.ShapeDtypeStruct((PATCH * PATCH, LANES), jnp.float32),
            jax.ShapeDtypeStruct((LANES, 2 * LANES), jnp.float32),
            jax.ShapeDtypeStruct((HALF * HALF, 2 * LANES), jnp.float32),
        ],
        in_specs=[smem, smem, pl.BlockSpec(memory_space=pltpu.HBM), vmem, vmem],
        out_specs=[vmem] * 3,
        scratch_shapes=[
            VMEM((NPZ, PATCH, PATCH, PATCH), jnp.float32),
            VMEM((PATCH * PATCH, LANES), jnp.float32),
            pltpu.SemaphoreType.DMA((NPZ,)),
        ],
        compiler_params=pltpu.CompilerParams(vmem_limit_bytes=50 * 2**20),
        cost_estimate=pl.CostEstimate(flops=400_000_000, bytes_accessed=8_000_000, transcendentals=0),
        name="prepare",
    )(index, shift, bank, z_table(), rhs)


PITCH = 40


def patches_kernel(window_ref, spectra_ref, own_ref, b10, b01, b11,
                   o10, upper, near_ref, energy_ref, real, imag):
    window = halves(window_ref[...])

    for xq, yq, block in ((0, 0, None), (1, 0, b10), (0, 1, b01), (1, 1, b11)):
        if block is None:
            result = own_ref[...]
        else:
            result = dot3(halves(block[...].reshape(HALF * HALF, LANES)), window, 0)
        for i in range(HALF):
            rows = pl.ds((HALF * xq + i) * PITCH + HALF * yq, HALF)
            real[rows, :] = result[HALF * i : HALF * (i + 1), :LANES]
            imag[rows, :] = result[HALF * i : HALF * (i + 1), LANES:]

    def strided(h, y):
        return pl.ds(SUB * PITCH * h + y, SUB, stride=PITCH)

    for h in range(4):
        out = dft32(lambda y: (real[strided(h, y), :] * TAPER[y], imag[strided(h, y), :] * TAPER[y]), -1)
        for k, (re, im) in enumerate(out):
            real[strided(h, k), :] = re
            imag[strided(h, k), :] = im

    energy = jnp.zeros((SUB, LANES), jnp.float32)
    for g in range(4):
        def rows(x):
            return pl.ds(x * PITCH + SUB * g, SUB)

        out = dft32(lambda x: (real[rows(x), :] * TAPER[x], imag[rows(x), :] * TAPER[x]), -1)
        scaled = []
        for k, (re, im) in enumerate(out):
            s = spectra_ref[pl.ds(k * PATCH + SUB * g, SUB), :]
            sre, sim = s * re, s * im
            energy = energy + (sre * re + sim * im)
            scaled.append((sre, sim))
        out = dft32(lambda k: scaled[k], 1)
        for x, (re, im) in enumerate(out):
            real[rows(x), :] = re * (TAPER[x] / PATCH**3)
            imag[rows(x), :] = im * (TAPER[x] / PATCH**3)
    energy_ref[...] = energy

    for h in range(4):
        out = dft32(lambda k: (real[strided(h, k), :], imag[strided(h, k), :]), 1)
        for y, (re, im) in enumerate(out):
            real[strided(h, y), :] = re * TAPER[y]
            imag[strided(h, y), :] = im * TAPER[y]

    for xq, yq in ((0, 0), (0, 1), (1, 1), (1, 0)):
        pieces = []
        for i in range(HALF):
            rows = pl.ds((HALF * xq + i) * PITCH + HALF * yq, HALF)
            pieces.append(jnp.concatenate([real[rows, :], imag[rows, :]], axis=1))
        both = jnp.concatenate(pieces, axis=0)
        if xq == 0 and yq == 0:
            near_ref[...] = both
            continue
        image = dot3(halves(both), window, 1).reshape(HALF, HALF, LANES)
        if yq == 0:
            o10[...] = image
        else:
            upper[pl.ds(HALF * xq, HALF)] = image


def patches(window, spectra, own, blocks):
    block = jax.ShapeDtypeStruct(blocks[0].shape, jnp.float32)
    vmem = pl.BlockSpec(memory_space=VMEM)
    return pl.pallas_call(
        patches_kernel,
        out_shape=[block, jax.ShapeDtypeStruct((PATCH, HALF, LANES), jnp.float32)]
        + [jax.ShapeDtypeStruct(own.shape, jnp.float32), jax.ShapeDtypeStruct((SUB, LANES), jnp.float32)],
        in_specs=[vmem] * 6,
        out_specs=[vmem] * 4,
        scratch_shapes=[VMEM((PATCH * PITCH, LANES), jnp.float32)] * 2,
        compiler_params=pltpu.CompilerParams(vmem_limit_bytes=32 * 2**20),
        cost_estimate=pl.CostEstimate(flops=800_000_000, bytes_accessed=4_000_000, transcendentals=0),
        name="patches",
    )(window, spectra, own, *blocks)


def near_kernel(window_ref, near_ref, energy_ref, rhs_ref, damping_ref, image_ref, sums_ref):
    field = rhs_ref[...]
    square = field * field
    damped = damping_ref[...]
    rr = jnp.sum(square)
    dd = jnp.sum(square * damped) + jnp.sum(energy_ref[...]) * (1.0 / PATCH**3)
    lane = lax.broadcasted_iota(jnp.int32, sums_ref.shape, len(sums_ref.shape) - 1)
    sums_ref[...] = jnp.where(lane == 0, rr, jnp.where(lane == 1, dd, 0.0))
    own = dot3(halves(near_ref[...]), halves(window_ref[...]), 1)
    image_ref[...] = own.reshape(field.shape) + damped * field


def near(window, inner, energy, rhs, damping):
    vmem = pl.BlockSpec(memory_space=VMEM)
    return pl.pallas_call(
        near_kernel,
        out_shape=[
            jax.ShapeDtypeStruct(rhs.shape, jnp.float32),
            jax.ShapeDtypeStruct((256, 1, LANES), jnp.float32),
        ],
        in_specs=[vmem] * 5,
        out_specs=[vmem] * 2,
        compiler_params=pltpu.CompilerParams(vmem_limit_bytes=32 * 2**20),
        cost_estimate=pl.CostEstimate(flops=20_000_000_000, bytes_accessed=40_000_000, transcendentals=0),
        name="near",
    )(window, inner, energy, rhs, damping)


def finish_kernel(sums_ref, rhs_ref, own, from_y, from_x, solution_ref, residual_ref):
    totals = jnp.sum(sums_ref[...], axis=(0, 1), keepdims=True)[0]
    lane = lax.broadcasted_iota(jnp.int32, totals.shape, 1)
    rr = jnp.sum(jnp.where(lane == 0, totals, 0.0), axis=1, keepdims=True)
    dd = jnp.sum(jnp.where(lane == 1, totals, 0.0), axis=1, keepdims=True)
    alpha = (rr / dd)[None]
    rhs = rhs_ref[...]
    image = (own[...] + from_y[:HALF]) + from_x[...]
    solution_ref[...] = alpha * rhs
    residual_ref[...] = rhs - alpha * image


def finish(sums, rhs, parts):
    block = jax.ShapeDtypeStruct(rhs.shape, jnp.float32)
    vmem = pl.BlockSpec(memory_space=VMEM)
    return pl.pallas_call(
        finish_kernel,
        out_shape=[block, block],
        in_specs=[vmem] * 5,
        out_specs=[vmem] * 2,
        compiler_params=pltpu.CompilerParams(vmem_limit_bytes=8 * 2**20),
        cost_estimate=pl.CostEstimate(flops=1_000_000, bytes_accessed=1_000_000, transcendentals=0),
        name="finish",
    )(sums, rhs, *parts)


def moved(x, by_x, by_y):
    nx, ny = lax.axis_size("gx"), lax.axis_size("gy")
    pairs = [
        (i * ny + j, (i + by_x) * ny + j + by_y)
        for i in range(nx)
        for j in range(ny)
        if 0 <= i + by_x < nx and 0 <= j + by_y < ny
    ]
    return lax.ppermute(x, ("gx", "gy"), pairs)


def body(migrated, prior_sample, damping, psf_bank, psf_index, z_shift):
    rhs = migrated + damping * prior_sample
    halo = [moved(rhs, -1, 0), moved(rhs, 0, -1), moved(rhs, -1, -1)]
    spectra, window, own = prepare(psf_index.reshape(NPZ), z_shift.reshape(1), psf_bank, rhs)
    o10, upper, inner, energy = patches(window, spectra, own, halo)
    from_y = moved(upper, 0, 1)
    image, sums = near(window, inner, energy, rhs, damping)
    sums = lax.all_to_all(sums, ("gx", "gy"), 0, 0)
    from_x = moved(o10 + from_y[HALF:], 1, 0)
    return tuple(finish(sums, rhs, [image, from_y, from_x]))


def solution(mesh):
    block = P("gx", "gy", None)
    return jax.shard_map(
        body,
        mesh=mesh,
        in_specs=(block, block, block, P(), block, P("gx", "gy")),
        out_specs=(block, block),
        check_vma=False,
    )
```

```python
import math

import jax
import jax.numpy as jnp
from jax import lax
from jax.experimental import pallas as pl
from jax.experimental.pallas import tpu as pltpu
from jax.sharding import PartitionSpec as P

PATCH = 32
HALF = 16
NPZ = 6
KZ = 17
LANES = 128
SUB = 8
VMEM = pltpu.VMEM


TAPER = [math.sin(math.pi * (i + 0.5) / PATCH) for i in range(PATCH)]


def twiddle(value, k, n, sign):
    k %= n
    re, im = value
    if k == 0:
        return value
    if 4 * k == n:
        return (-im, re) if sign > 0 else (im, -re)
    if 2 * k == n:
        return (-re, -im)
    if 4 * k == 3 * n:
        return (im, -re) if sign > 0 else (-im, re)
    c = math.cos(2.0 * math.pi * k / n)
    s = sign * math.sin(2.0 * math.pi * k / n)
    if 8 * k % n == 0:
        h = abs(c)
        cs, ss = (1 if c > 0 else -1), (1 if s > 0 else -1)
        if cs == ss:
            a, b = re - im, re + im
            return (a * (h * cs), b * (h * cs))
        a, b = re + im, im - re
        return (a * (h * cs), b * (h * cs))
    return (re * c - im * s, re * s + im * c)


def add(a, b):
    return (a[0] + b[0], a[1] + b[1])


def sub(a, b):
    return (a[0] - b[0], a[1] - b[1])


def dft4(x, sign):
    a, b = add(x[0], x[2]), sub(x[0], x[2])
    c, d = add(x[1], x[3]), twiddle(sub(x[1], x[3]), 1, 4, sign)
    return [add(a, c), add(b, d), sub(a, c), sub(b, d)]


def dft8(x, sign):
    even = dft4(x[0::2], sign)
    odd = [twiddle(v, k, 8, sign) for k, v in enumerate(dft4(x[1::2], sign))]
    return [add(even[k], odd[k]) for k in range(4)] + [sub(even[k], odd[k]) for k in range(4)]


def dft32(load, sign):
    first = []
    for n2 in range(8):
        part = dft4([load(8 * n1 + n2) for n1 in range(4)], sign)
        first.append([twiddle(v, n2 * k1, 32, sign) for k1, v in enumerate(part)])
    out = [None] * 32
    for k1 in range(4):
        part = dft8([first[n2][k1] for n2 in range(8)], sign)
        for k2 in range(8):
            out[k1 + 4 * k2] = part[k2]
    return out


def halves(value):
    high = value.astype(jnp.bfloat16)
    return high, (value - high.astype(jnp.float32)).astype(jnp.bfloat16)


def dot(a, b, contract_b):
    return lax.dot_general(a, b, (((1,), (contract_b,)), ((), ())), preferred_element_type=jnp.float32)


def dot3(a, b, contract_b):
    return dot(a[0], b[0], contract_b) + (dot(a[1], b[0], contract_b) + dot(a[0], b[1], contract_b))


def lookup(values, places):
    lane = lax.broadcasted_iota(jnp.int32, (SUB, LANES), 1)
    table = jnp.zeros((SUB, LANES), jnp.float32)
    for i, value in enumerate(values):
        table = jnp.where(lane == i, value, table)
    return jnp.take_along_axis(table, places, axis=1, mode="promise_in_bounds")


COSINES = [math.cos(2.0 * math.pi * i / PATCH) for i in range(PATCH)]
COSINES[8] = COSINES[24] = 0.0


def window_of(shift, window_ref):
    lane = lax.broadcasted_iota(jnp.int32, (SUB, LANES), 1)
    p = jnp.zeros_like(lane)
    for q in range(1, NPZ):
        p = jnp.where(lane >= KZ * q, q, p)
    kz = lane - KZ * p
    first = lax.broadcasted_iota(jnp.int32, (SUB, LANES), 0) - shift - HALF * p
    for g in range(LANES // SUB):
        cell = first + SUB * g
        inside = (cell >= 0) & (cell < PATCH) & (lane < KZ * NPZ)
        cell = cell & (PATCH - 1)
        taper = jnp.where(inside, lookup(TAPER, cell), 0.0)
        phase = (kz * cell) & (PATCH - 1)
        rows = pl.ds(SUB * g, SUB)
        window_ref[rows, :LANES] = taper * lookup(COSINES, phase)
        sine = taper * lookup(COSINES, (phase + PATCH // 4) & (PATCH - 1))
        window_ref[rows, LANES:] = jnp.where((kz == 0) | (kz == HALF), 0.0, sine)


def prepare_kernel(index_ref, shift_ref, bank_ref, block_ref,
                   spectra_ref, window_ref, own_ref, cubes, back, sems):
    copies = [
        pltpu.make_async_copy(bank_ref.at[index_ref[0, 0, p]], cubes.at[p], sems.at[p]) for p in range(NPZ)
    ]
    for copy in copies:
        copy.start()

    window_of(shift_ref[0, 0], window_ref)
    own_ref[...] = dot3(halves(block_ref[...].reshape(HALF * HALF, LANES)), halves(window_ref[...]), 0)

    source = lax.broadcasted_iota(jnp.int32, (NPZ * PATCH, 2 * LANES), 0)
    lane = lax.broadcasted_iota(jnp.int32, (NPZ * PATCH, 2 * LANES), 1)
    p, kz = source // PATCH, source % PATCH
    target = jnp.where(kz < KZ, KZ * p + kz, LANES + KZ * p + PATCH - kz)
    pick = jnp.where(lane == target, 1.0, 0.0).astype(jnp.bfloat16)

    for copy in copies:
        copy.wait()
    total = None
    for first, last in ((0, 4), (4, NPZ)):
        joined = jnp.concatenate(
            [cubes[q].reshape(PATCH * PATCH, PATCH) for q in range(first, last)], axis=1
        )
        high, low = halves(joined)
        rows = pick[PATCH * first : PATCH * last]
        part = dot(high, rows, 0) + dot(low, rows, 0)
        total = part if total is None else total + part
    spectra_ref[...] = total[:, :LANES]
    back[...] = total[:, LANES:]
    row = lax.broadcasted_iota(jnp.int32, (SUB, LANES), 0)
    mirror = (SUB - row) % SUB
    for kx in range(PATCH):
        other = (PATCH - kx) % PATCH
        turned = [
            jnp.take_along_axis(
                back[pl.ds(other * PATCH + SUB * g, SUB), :], mirror, axis=0, mode="promise_in_bounds"
            )
            for g in range(4)
        ]
        for g in range(4):
            rows = pl.ds(kx * PATCH + SUB * g, SUB)
            mirrored = jnp.where(row == 0, turned[(4 - g) % 4], turned[3 - g])
            spectra_ref[rows, :] = spectra_ref[rows, :] + mirrored


def prepare(index, shift, bank, rhs):
    smem = pl.BlockSpec(memory_space=pltpu.SMEM)
    vmem = pl.BlockSpec(memory_space=VMEM)
    return pl.pallas_call(
        prepare_kernel,
        out_shape=[
            jax.ShapeDtypeStruct((PATCH * PATCH, LANES), jnp.float32),
            jax.ShapeDtypeStruct((LANES, 2 * LANES), jnp.float32),
            jax.ShapeDtypeStruct((HALF * HALF, 2 * LANES), jnp.float32),
        ],
        in_specs=[smem, smem, pl.BlockSpec(memory_space=pltpu.HBM), vmem],
        out_specs=[vmem] * 3,
        scratch_shapes=[
            VMEM((NPZ, PATCH, PATCH, PATCH), jnp.float32),
            VMEM((PATCH * PATCH, LANES), jnp.float32),
            pltpu.SemaphoreType.DMA((NPZ,)),
        ],
        compiler_params=pltpu.CompilerParams(vmem_limit_bytes=50 * 2**20),
        cost_estimate=pl.CostEstimate(flops=400_000_000, bytes_accessed=8_000_000, transcendentals=0),
        name="prepare",
    )(index, shift, bank, rhs)


PITCH = 40


def patches_kernel(window_ref, spectra_ref, own_ref, b10, b01, b11,
                   o10, upper, near_ref, energy_ref, real, imag):
    window = halves(window_ref[...])

    for xq, yq, block in ((0, 0, None), (1, 0, b10), (0, 1, b01), (1, 1, b11)):
        if block is None:
            result = own_ref[...]
        else:
            result = dot3(halves(block[...].reshape(HALF * HALF, LANES)), window, 0)
        for i in range(HALF):
            rows = pl.ds((HALF * xq + i) * PITCH + HALF * yq, HALF)
            real[rows, :] = result[HALF * i : HALF * (i + 1), :LANES]
            imag[rows, :] = result[HALF * i : HALF * (i + 1), LANES:]

    def strided(h, y):
        return pl.ds(SUB * PITCH * h + y, SUB, stride=PITCH)

    for h in range(4):
        out = dft32(lambda y: (real[strided(h, y), :] * TAPER[y], imag[strided(h, y), :] * TAPER[y]), -1)
        for k, (re, im) in enumerate(out):
            real[strided(h, k), :] = re
            imag[strided(h, k), :] = im

    energy = jnp.zeros((SUB, LANES), jnp.float32)
    for g in range(4):
        def rows(x):
            return pl.ds(x * PITCH + SUB * g, SUB)

        out = dft32(lambda x: (real[rows(x), :] * TAPER[x], imag[rows(x), :] * TAPER[x]), -1)
        scaled = []
        for k, (re, im) in enumerate(out):
            s = spectra_ref[pl.ds(k * PATCH + SUB * g, SUB), :]
            sre, sim = s * re, s * im
            energy = energy + (sre * re + sim * im)
            scaled.append((sre, sim))
        out = dft32(lambda k: scaled[k], 1)
        for x, (re, im) in enumerate(out):
            real[rows(x), :] = re * (TAPER[x] / PATCH**3)
            imag[rows(x), :] = im * (TAPER[x] / PATCH**3)
    energy_ref[...] = energy

    for h in range(4):
        out = dft32(lambda k: (real[strided(h, k), :], imag[strided(h, k), :]), 1)
        for y, (re, im) in enumerate(out):
            real[strided(h, y), :] = re * TAPER[y]
            imag[strided(h, y), :] = im * TAPER[y]

    for xq, yq in ((0, 0), (0, 1), (1, 1), (1, 0)):
        pieces = []
        for i in range(HALF):
            rows = pl.ds((HALF * xq + i) * PITCH + HALF * yq, HALF)
            pieces.append(jnp.concatenate([real[rows, :], imag[rows, :]], axis=1))
        both = jnp.concatenate(pieces, axis=0)
        if xq == 0 and yq == 0:
            near_ref[...] = both
            continue
        image = dot3(halves(both), window, 1).reshape(HALF, HALF, LANES)
        if yq == 0:
            o10[...] = image
        else:
            upper[pl.ds(HALF * xq, HALF)] = image


def patches(window, spectra, own, blocks):
    block = jax.ShapeDtypeStruct(blocks[0].shape, jnp.float32)
    vmem = pl.BlockSpec(memory_space=VMEM)
    return pl.pallas_call(
        patches_kernel,
        out_shape=[block, jax.ShapeDtypeStruct((PATCH, HALF, LANES), jnp.float32)]
        + [jax.ShapeDtypeStruct(own.shape, jnp.float32), jax.ShapeDtypeStruct((SUB, LANES), jnp.float32)],
        in_specs=[vmem] * 6,
        out_specs=[vmem] * 4,
        scratch_shapes=[VMEM((PATCH * PITCH, LANES), jnp.float32)] * 2,
        compiler_params=pltpu.CompilerParams(vmem_limit_bytes=32 * 2**20),
        cost_estimate=pl.CostEstimate(flops=800_000_000, bytes_accessed=4_000_000, transcendentals=0),
        name="patches",
    )(window, spectra, own, *blocks)


def near_kernel(window_ref, near_ref, energy_ref, rhs_ref, damping_ref, image_ref, sums_ref):
    field = rhs_ref[...]
    square = field * field
    damped = damping_ref[...]
    rr = jnp.sum(square)
    dd = jnp.sum(square * damped) + jnp.sum(energy_ref[...]) * (1.0 / PATCH**3)
    lane = lax.broadcasted_iota(jnp.int32, sums_ref.shape, len(sums_ref.shape) - 1)
    sums_ref[...] = jnp.where(lane == 0, rr, jnp.where(lane == 1, dd, 0.0))
    own = dot3(halves(near_ref[...]), halves(window_ref[...]), 1)
    image_ref[...] = own.reshape(field.shape) + damped * field


def near(window, inner, energy, rhs, damping, copies):
    vmem = pl.BlockSpec(memory_space=VMEM)
    return pl.pallas_call(
        near_kernel,
        out_shape=[
            jax.ShapeDtypeStruct(rhs.shape, jnp.float32),
            jax.ShapeDtypeStruct((copies, 1, LANES), jnp.float32),
        ],
        in_specs=[vmem] * 5,
        out_specs=[vmem] * 2,
        compiler_params=pltpu.CompilerParams(vmem_limit_bytes=32 * 2**20),
        cost_estimate=pl.CostEstimate(flops=20_000_000_000, bytes_accessed=40_000_000, transcendentals=0),
        name="near",
    )(window, inner, energy, rhs, damping)


def finish_kernel(sums_ref, others_ref, rhs_ref, own, from_y, from_x, solution_ref, residual_ref):
    totals = [jnp.sum(ref[...], axis=(0, 1), keepdims=True)[0] for ref in (sums_ref, others_ref)]
    totals = totals[0] + totals[1]
    lane = lax.broadcasted_iota(jnp.int32, totals.shape, 1)
    rr = jnp.sum(jnp.where(lane == 0, totals, 0.0), axis=1, keepdims=True)
    dd = jnp.sum(jnp.where(lane == 1, totals, 0.0), axis=1, keepdims=True)
    alpha = (rr / dd)[None]
    rhs = rhs_ref[...]
    image = (own[...] + from_y[:HALF]) + from_x[...]
    solution_ref[...] = alpha * rhs
    residual_ref[...] = rhs - alpha * image


def finish(sums, others, rhs, parts):
    block = jax.ShapeDtypeStruct(rhs.shape, jnp.float32)
    vmem = pl.BlockSpec(memory_space=VMEM)
    return pl.pallas_call(
        finish_kernel,
        out_shape=[block, block],
        in_specs=[vmem] * 6,
        out_specs=[vmem] * 2,
        compiler_params=pltpu.CompilerParams(vmem_limit_bytes=8 * 2**20),
        cost_estimate=pl.CostEstimate(flops=1_000_000, bytes_accessed=1_000_000, transcendentals=0),
        name="finish",
    )(sums, others, rhs, *parts)


def moved(x, by_x, by_y):
    nx, ny = lax.axis_size("gx"), lax.axis_size("gy")
    pairs = [
        (i * ny + j, (i + by_x) * ny + j + by_y)
        for i in range(nx)
        for j in range(ny)
        if 0 <= i + by_x < nx and 0 <= j + by_y < ny
    ]
    return lax.ppermute(x, ("gx", "gy"), pairs)


def body(migrated, prior_sample, damping, psf_bank, psf_index, z_shift):
    rhs = migrated + damping * prior_sample
    nx, ny = lax.axis_size("gx"), lax.axis_size("gy")
    halo = [moved(rhs, -1, 0), moved(rhs, 0, -1), moved(rhs, -1, -1)]
    spectra, window, own = prepare(psf_index, z_shift, psf_bank, rhs)
    o10, upper, inner, energy = patches(window, spectra, own, halo)
    from_y = moved(upper, 0, 1)
    image, sums = near(window, inner, energy, rhs, damping, nx * ny // 2)
    groups = [[i * ny + j for i in range(nx) for j in range(k, ny, 2)] for k in range(2)]
    sums = lax.all_to_all(sums, ("gx", "gy"), 0, 0, axis_index_groups=groups)
    others = lax.ppermute(sums, "gy", [(j, j ^ 1) for j in range(ny)])
    from_x = moved(o10 + from_y[HALF:], 1, 0)
    return tuple(finish(sums, others, rhs, [image, from_y, from_x]))


def solution(mesh):
    block = P("gx", "gy", None)
    return jax.shard_map(
        body,
        mesh=mesh,
        in_specs=(block, block, block, P(), block, P("gx", "gy")),
        out_specs=(block, block),
        check_vma=False,
    )
```

```python
import math

import jax
import jax.numpy as jnp
from jax import lax
from jax.experimental import pallas as pl
from jax.experimental.pallas import tpu as pltpu
from jax.sharding import PartitionSpec as P

PATCH = 32
HALF = 16
NPZ = 6
KZ = 17
LANES = 128
SUB = 8
VMEM = pltpu.VMEM


TAPER = [math.sin(math.pi * (i + 0.5) / PATCH) for i in range(PATCH)]


def twiddle(value, k, n, sign):
    k %= n
    re, im = value
    if k == 0:
        return value
    if 4 * k == n:
        return (-im, re) if sign > 0 else (im, -re)
    if 2 * k == n:
        return (-re, -im)
    if 4 * k == 3 * n:
        return (im, -re) if sign > 0 else (-im, re)
    c = math.cos(2.0 * math.pi * k / n)
    s = sign * math.sin(2.0 * math.pi * k / n)
    if 8 * k % n == 0:
        h = abs(c)
        cs, ss = (1 if c > 0 else -1), (1 if s > 0 else -1)
        if cs == ss:
            a, b = re - im, re + im
            return (a * (h * cs), b * (h * cs))
        a, b = re + im, im - re
        return (a * (h * cs), b * (h * cs))
    return (re * c - im * s, re * s + im * c)


def add(a, b):
    return (a[0] + b[0], a[1] + b[1])


def sub(a, b):
    return (a[0] - b[0], a[1] - b[1])


def dft4(x, sign):
    a, b = add(x[0], x[2]), sub(x[0], x[2])
    c, d = add(x[1], x[3]), twiddle(sub(x[1], x[3]), 1, 4, sign)
    return [add(a, c), add(b, d), sub(a, c), sub(b, d)]


def dft8(x, sign):
    even = dft4(x[0::2], sign)
    odd = [twiddle(v, k, 8, sign) for k, v in enumerate(dft4(x[1::2], sign))]
    return [add(even[k], odd[k]) for k in range(4)] + [sub(even[k], odd[k]) for k in range(4)]


def dft32(load, sign):
    first = []
    for n2 in range(8):
        part = dft4([load(8 * n1 + n2) for n1 in range(4)], sign)
        first.append([twiddle(v, n2 * k1, 32, sign) for k1, v in enumerate(part)])
    out = [None] * 32
    for k1 in range(4):
        part = dft8([first[n2][k1] for n2 in range(8)], sign)
        for k2 in range(8):
            out[k1 + 4 * k2] = part[k2]
    return out


def halves(value):
    high = value.astype(jnp.bfloat16)
    return high, (value - high.astype(jnp.float32)).astype(jnp.bfloat16)


def dot(a, b, contract_b):
    return lax.dot_general(a, b, (((1,), (contract_b,)), ((), ())), preferred_element_type=jnp.float32)


def dot3(a, b, contract_b):
    return dot(a[0], b[0], contract_b) + (dot(a[1], b[0], contract_b) + dot(a[0], b[1], contract_b))


def lookup(values, places):
    lane = lax.broadcasted_iota(jnp.int32, (SUB, LANES), 1)
    table = jnp.zeros((SUB, LANES), jnp.float32)
    for i, value in enumerate(values):
        table = jnp.where(lane == i, value, table)
    return jnp.take_along_axis(table, places, axis=1, mode="promise_in_bounds")


COSINES = [math.cos(2.0 * math.pi * i / PATCH) for i in range(PATCH)]
COSINES[8] = COSINES[24] = 0.0


def window_of(shift, window_ref):
    lane = lax.broadcasted_iota(jnp.int32, (SUB, LANES), 1)
    p = jnp.zeros_like(lane)
    for q in range(1, NPZ):
        p = jnp.where(lane >= KZ * q, q, p)
    kz = lane - KZ * p
    first = lax.broadcasted_iota(jnp.int32, (SUB, LANES), 0) - shift - HALF * p
    for g in range(LANES // SUB):
        cell = first + SUB * g
        inside = (cell >= 0) & (cell < PATCH) & (lane < KZ * NPZ)
        cell = cell & (PATCH - 1)
        taper = jnp.where(inside, lookup(TAPER, cell), 0.0)
        phase = (kz * cell) & (PATCH - 1)
        rows = pl.ds(SUB * g, SUB)
        window_ref[rows, :LANES] = taper * lookup(COSINES, phase)
        sine = taper * lookup(COSINES, (phase + PATCH // 4) & (PATCH - 1))
        window_ref[rows, LANES:] = jnp.where((kz == 0) | (kz == HALF), 0.0, sine)


def prepare_kernel(index_ref, shift_ref, bank_ref, block_ref,
                   spectra_ref, window_ref, own_ref, cubes, back, sems):
    copies = [
        pltpu.make_async_copy(bank_ref.at[index_ref[0, 0, p]], cubes.at[p], sems.at[p]) for p in range(NPZ)
    ]
    for copy in copies:
        copy.start()

    window_of(shift_ref[0, 0], window_ref)
    own_ref[...] = dot3(halves(block_ref[...].reshape(HALF * HALF, LANES)), halves(window_ref[...]), 0)

    source = lax.broadcasted_iota(jnp.int32, (NPZ * PATCH, 2 * LANES), 0)
    lane = lax.broadcasted_iota(jnp.int32, (NPZ * PATCH, 2 * LANES), 1)
    p, kz = source // PATCH, source % PATCH
    target = jnp.where(kz < KZ, KZ * p + kz, LANES + KZ * p + PATCH - kz)
    pick = jnp.where(lane == target, 1.0, 0.0).astype(jnp.bfloat16)

    for copy in copies:
        copy.wait()
    total = None
    for first, last in ((0, 4), (4, NPZ)):
        joined = jnp.concatenate(
            [cubes[q].reshape(PATCH * PATCH, PATCH) for q in range(first, last)], axis=1
        )
        high, low = halves(joined)
        rows = pick[PATCH * first : PATCH * last]
        part = dot(high, rows, 0) + dot(low, rows, 0)
        total = part if total is None else total + part
    spectra_ref[...] = total[:, :LANES]
    back[...] = total[:, LANES:]
    row = lax.broadcasted_iota(jnp.int32, (SUB, LANES), 0)
    mirror = (SUB - row) % SUB
    for kx in range(PATCH):
        other = (PATCH - kx) % PATCH
        turned = [
            jnp.take_along_axis(
                back[pl.ds(other * PATCH + SUB * g, SUB), :], mirror, axis=0, mode="promise_in_bounds"
            )
            for g in range(4)
        ]
        for g in range(4):
            rows = pl.ds(kx * PATCH + SUB * g, SUB)
            mirrored = jnp.where(row == 0, turned[(4 - g) % 4], turned[3 - g])
            spectra_ref[rows, :] = spectra_ref[rows, :] + mirrored


def prepare(index, shift, bank, rhs):
    smem = pl.BlockSpec(memory_space=pltpu.SMEM)
    vmem = pl.BlockSpec(memory_space=VMEM)
    return pl.pallas_call(
        prepare_kernel,
        out_shape=[
            jax.ShapeDtypeStruct((PATCH * PATCH, LANES), jnp.float32),
            jax.ShapeDtypeStruct((LANES, 2 * LANES), jnp.float32),
            jax.ShapeDtypeStruct((HALF * HALF, 2 * LANES), jnp.float32),
        ],
        in_specs=[smem, smem, pl.BlockSpec(memory_space=pltpu.HBM), vmem],
        out_specs=[vmem] * 3,
        scratch_shapes=[
            VMEM((NPZ, PATCH, PATCH, PATCH), jnp.float32),
            VMEM((PATCH * PATCH, LANES), jnp.float32),
            pltpu.SemaphoreType.DMA((NPZ,)),
        ],
        compiler_params=pltpu.CompilerParams(vmem_limit_bytes=50 * 2**20),
        cost_estimate=pl.CostEstimate(flops=400_000_000, bytes_accessed=8_000_000, transcendentals=0),
        name="prepare",
    )(index, shift, bank, rhs)


PITCH = 40


def patches_kernel(window_ref, spectra_ref, own_ref, rhs_ref, damping_ref, b10, b01, b11,
                   o10, upper, near_ref, sums_ref, real, imag, sums, sem):
    window = halves(window_ref[...])

    for xq, yq, block in ((0, 0, None), (1, 0, b10), (0, 1, b01), (1, 1, b11)):
        if block is None:
            result = own_ref[...]
        else:
            result = dot3(halves(block[...].reshape(HALF * HALF, LANES)), window, 0)
        for i in range(HALF):
            rows = pl.ds((HALF * xq + i) * PITCH + HALF * yq, HALF)
            real[rows, :] = result[HALF * i : HALF * (i + 1), :LANES]
            imag[rows, :] = result[HALF * i : HALF * (i + 1), LANES:]

    def strided(h, y):
        return pl.ds(SUB * PITCH * h + y, SUB, stride=PITCH)

    for h in range(4):
        out = dft32(lambda y: (real[strided(h, y), :] * TAPER[y], imag[strided(h, y), :] * TAPER[y]), -1)
        for k, (re, im) in enumerate(out):
            real[strided(h, k), :] = re
            imag[strided(h, k), :] = im

    energy = jnp.zeros((SUB, LANES), jnp.float32)
    for g in range(4):
        def rows(x):
            return pl.ds(x * PITCH + SUB * g, SUB)

        out = dft32(lambda x: (real[rows(x), :] * TAPER[x], imag[rows(x), :] * TAPER[x]), -1)
        scaled = []
        for k, (re, im) in enumerate(out):
            s = spectra_ref[pl.ds(k * PATCH + SUB * g, SUB), :]
            sre, sim = s * re, s * im
            energy = energy + (sre * re + sim * im)
            scaled.append((sre, sim))
        out = dft32(lambda k: scaled[k], 1)
        for x, (re, im) in enumerate(out):
            real[rows(x), :] = re * (TAPER[x] / PATCH**3)
            imag[rows(x), :] = im * (TAPER[x] / PATCH**3)

    square = rhs_ref[...] * rhs_ref[...]
    rr = jnp.sum(square)
    dd = jnp.sum(square * damping_ref[...]) + jnp.sum(energy) * (1.0 / PATCH**3)
    lane = lax.broadcasted_iota(jnp.int32, sums.shape, len(sums.shape) - 1)
    sums[...] = jnp.where(lane == 0, rr, jnp.where(lane == 1, dd, 0.0))
    leaving = pltpu.make_async_copy(sums, sums_ref, sem)
    leaving.start()

    for h in range(4):
        out = dft32(lambda k: (real[strided(h, k), :], imag[strided(h, k), :]), 1)
        for y, (re, im) in enumerate(out):
            real[strided(h, y), :] = re * TAPER[y]
            imag[strided(h, y), :] = im * TAPER[y]

    for xq, yq in ((0, 0), (0, 1), (1, 1), (1, 0)):
        pieces = []
        for i in range(HALF):
            rows = pl.ds((HALF * xq + i) * PITCH + HALF * yq, HALF)
            pieces.append(jnp.concatenate([real[rows, :], imag[rows, :]], axis=1))
        both = jnp.concatenate(pieces, axis=0)
        if xq == 0 and yq == 0:
            near_ref[...] = both
            continue
        image = dot3(halves(both), window, 1).reshape(HALF, HALF, LANES)
        if yq == 0:
            o10[...] = image
        else:
            upper[pl.ds(HALF * xq, HALF)] = image
    leaving.wait()


def patches(window, spectra, own, rhs, damping, blocks, copies):
    block = jax.ShapeDtypeStruct(blocks[0].shape, jnp.float32)
    vmem = pl.BlockSpec(memory_space=VMEM)
    return pl.pallas_call(
        patches_kernel,
        out_shape=[block, jax.ShapeDtypeStruct((PATCH, HALF, LANES), jnp.float32)]
        + [jax.ShapeDtypeStruct(own.shape, jnp.float32), jax.ShapeDtypeStruct((copies, 1, LANES), jnp.float32)],
        in_specs=[vmem] * 8,
        out_specs=[vmem] * 3 + [pl.BlockSpec(memory_space=pltpu.HBM)],
        scratch_shapes=[VMEM((PATCH * PITCH, LANES), jnp.float32)] * 2
        + [VMEM((copies, 1, LANES), jnp.float32), pltpu.SemaphoreType.DMA],
        compiler_params=pltpu.CompilerParams(vmem_limit_bytes=32 * 2**20),
        cost_estimate=pl.CostEstimate(flops=800_000_000, bytes_accessed=4_000_000, transcendentals=0),
        name="patches",
    )(window, spectra, own, rhs, damping, *blocks)


def near_kernel(window_ref, near_ref, rhs_ref, damping_ref, image_ref):
    own = dot3(halves(near_ref[...]), halves(window_ref[...]), 1)
    image_ref[...] = own.reshape(image_ref.shape) + damping_ref[...] * rhs_ref[...]


def near(window, inner, rhs, damping):
    vmem = pl.BlockSpec(memory_space=VMEM)
    return pl.pallas_call(
        near_kernel,
        out_shape=jax.ShapeDtypeStruct(rhs.shape, jnp.float32),
        in_specs=[vmem] * 4,
        out_specs=vmem,
        compiler_params=pltpu.CompilerParams(vmem_limit_bytes=32 * 2**20),
        cost_estimate=pl.CostEstimate(flops=20_000_000, bytes_accessed=1_000_000, transcendentals=0),
        name="near",
    )(window, inner, rhs, damping)


def finish_kernel(sums_ref, others_ref, rhs_ref, own, from_y, from_x, solution_ref, residual_ref):
    totals = [jnp.sum(ref[...], axis=(0, 1), keepdims=True)[0] for ref in (sums_ref, others_ref)]
    totals = totals[0] + totals[1]
    lane = lax.broadcasted_iota(jnp.int32, totals.shape, 1)
    rr = jnp.sum(jnp.where(lane == 0, totals, 0.0), axis=1, keepdims=True)
    dd = jnp.sum(jnp.where(lane == 1, totals, 0.0), axis=1, keepdims=True)
    alpha = (rr / dd)[None]
    rhs = rhs_ref[...]
    image = (own[...] + from_y[:HALF]) + from_x[...]
    solution_ref[...] = alpha * rhs
    residual_ref[...] = rhs - alpha * image


def finish(sums, others, rhs, parts):
    block = jax.ShapeDtypeStruct(rhs.shape, jnp.float32)
    vmem = pl.BlockSpec(memory_space=VMEM)
    return pl.pallas_call(
        finish_kernel,
        out_shape=[block, block],
        in_specs=[vmem] * 6,
        out_specs=[vmem] * 2,
        compiler_params=pltpu.CompilerParams(vmem_limit_bytes=8 * 2**20),
        cost_estimate=pl.CostEstimate(flops=1_000_000, bytes_accessed=1_000_000, transcendentals=0),
        name="finish",
    )(sums, others, rhs, *parts)


def moved(x, by_x, by_y):
    nx, ny = lax.axis_size("gx"), lax.axis_size("gy")
    pairs = [
        (i * ny + j, (i + by_x) * ny + j + by_y)
        for i in range(nx)
        for j in range(ny)
        if 0 <= i + by_x < nx and 0 <= j + by_y < ny
    ]
    return lax.ppermute(x, ("gx", "gy"), pairs)


def body(migrated, prior_sample, damping, psf_bank, psf_index, z_shift):
    rhs = migrated + damping * prior_sample
    nx, ny = lax.axis_size("gx"), lax.axis_size("gy")
    halo = [moved(rhs, -1, 0), moved(rhs, 0, -1), moved(rhs, -1, -1)]
    spectra, window, own = prepare(psf_index, z_shift, psf_bank, rhs)
    o10, upper, inner, sums = patches(window, spectra, own, rhs, damping, halo, nx * ny // 2)
    from_y = moved(upper, 0, 1)
    image = near(window, inner, rhs, damping)
    groups = [[i * ny + j for i in range(nx) for j in range(k, ny, 2)] for k in range(2)]
    sums = lax.all_to_all(sums, ("gx", "gy"), 0, 0, axis_index_groups=groups)
    others = lax.ppermute(sums, "gy", [(j, j ^ 1) for j in range(ny)])
    from_x = moved(o10 + from_y[HALF:], 1, 0)
    return tuple(finish(sums, others, rhs, [image, from_y, from_x]))


def solution(mesh):
    block = P("gx", "gy", None)
    return jax.shard_map(
        body,
        mesh=mesh,
        in_specs=(block, block, block, P(), block, P("gx", "gy")),
        out_specs=(block, block),
        check_vma=False,
    )
```

```python
import math

import jax
import jax.numpy as jnp
from jax import lax
from jax.experimental import pallas as pl
from jax.experimental.pallas import tpu as pltpu
from jax.sharding import PartitionSpec as P

PATCH = 32
HALF = 16
NPZ = 6
KZ = 17
LANES = 128
SUB = 8
VMEM = pltpu.VMEM


TAPER = [math.sin(math.pi * (i + 0.5) / PATCH) for i in range(PATCH)]


def twiddle(value, k, n, sign):
    k %= n
    re, im = value
    if k == 0:
        return value
    if 4 * k == n:
        return (-im, re) if sign > 0 else (im, -re)
    if 2 * k == n:
        return (-re, -im)
    if 4 * k == 3 * n:
        return (im, -re) if sign > 0 else (-im, re)
    c = math.cos(2.0 * math.pi * k / n)
    s = sign * math.sin(2.0 * math.pi * k / n)
    if 8 * k % n == 0:
        h = abs(c)
        cs, ss = (1 if c > 0 else -1), (1 if s > 0 else -1)
        if cs == ss:
            a, b = re - im, re + im
            return (a * (h * cs), b * (h * cs))
        a, b = re + im, im - re
        return (a * (h * cs), b * (h * cs))
    return (re * c - im * s, re * s + im * c)


def add(a, b):
    return (a[0] + b[0], a[1] + b[1])


def sub(a, b):
    return (a[0] - b[0], a[1] - b[1])


def dft4(x, sign):
    a, b = add(x[0], x[2]), sub(x[0], x[2])
    c, d = add(x[1], x[3]), twiddle(sub(x[1], x[3]), 1, 4, sign)
    return [add(a, c), add(b, d), sub(a, c), sub(b, d)]


def dft8(x, sign):
    even = dft4(x[0::2], sign)
    odd = [twiddle(v, k, 8, sign) for k, v in enumerate(dft4(x[1::2], sign))]
    return [add(even[k], odd[k]) for k in range(4)] + [sub(even[k], odd[k]) for k in range(4)]


def dft32(load, sign):
    first = []
    for n2 in range(8):
        part = dft4([load(8 * n1 + n2) for n1 in range(4)], sign)
        first.append([twiddle(v, n2 * k1, 32, sign) for k1, v in enumerate(part)])
    out = [None] * 32
    for k1 in range(4):
        part = dft8([first[n2][k1] for n2 in range(8)], sign)
        for k2 in range(8):
            out[k1 + 4 * k2] = part[k2]
    return out


def halves(value):
    high = value.astype(jnp.bfloat16)
    return high, (value - high.astype(jnp.float32)).astype(jnp.bfloat16)


def dot(a, b, contract_b):
    return lax.dot_general(a, b, (((1,), (contract_b,)), ((), ())), preferred_element_type=jnp.float32)


def dot3(a, b, contract_b):
    return dot(a[0], b[0], contract_b) + (dot(a[1], b[0], contract_b) + dot(a[0], b[1], contract_b))


def lookup(values, places):
    lane = lax.broadcasted_iota(jnp.int32, (SUB, LANES), 1)
    table = jnp.zeros((SUB, LANES), jnp.float32)
    for i, value in enumerate(values):
        table = jnp.where(lane == i, value, table)
    return jnp.take_along_axis(table, places, axis=1, mode="promise_in_bounds")


COSINES = [math.cos(2.0 * math.pi * i / PATCH) for i in range(PATCH)]
COSINES[8] = COSINES[24] = 0.0


def window_of(shift, window_ref):
    lane = lax.broadcasted_iota(jnp.int32, (SUB, LANES), 1)
    p = jnp.zeros_like(lane)
    for q in range(1, NPZ):
        p = jnp.where(lane >= KZ * q, q, p)
    kz = lane - KZ * p
    first = lax.broadcasted_iota(jnp.int32, (SUB, LANES), 0) - shift - HALF * p
    for g in range(LANES // SUB):
        cell = first + SUB * g
        inside = (cell >= 0) & (cell < PATCH) & (lane < KZ * NPZ)
        cell = cell & (PATCH - 1)
        taper = jnp.where(inside, lookup(TAPER, cell), 0.0)
        phase = (kz * cell) & (PATCH - 1)
        rows = pl.ds(SUB * g, SUB)
        window_ref[rows, :LANES] = taper * lookup(COSINES, phase)
        sine = taper * lookup(COSINES, (phase + PATCH // 4) & (PATCH - 1))
        window_ref[rows, LANES:] = jnp.where((kz == 0) | (kz == HALF), 0.0, sine)


def prepare_kernel(index_ref, shift_ref, bank_ref, block_ref,
                   spectra_ref, window_ref, own_ref, cubes, back, sems):
    copies = [
        pltpu.make_async_copy(bank_ref.at[index_ref[0, 0, p]], cubes.at[p], sems.at[p]) for p in range(NPZ)
    ]
    for copy in copies:
        copy.start()

    window_of(shift_ref[0, 0], window_ref)
    own_ref[...] = dot3(halves(block_ref[...].reshape(HALF * HALF, LANES)), halves(window_ref[...]), 0)

    source = lax.broadcasted_iota(jnp.int32, (NPZ * PATCH, 2 * LANES), 0)
    lane = lax.broadcasted_iota(jnp.int32, (NPZ * PATCH, 2 * LANES), 1)
    p, kz = source // PATCH, source % PATCH
    target = jnp.where(kz < KZ, KZ * p + kz, LANES + KZ * p + PATCH - kz)
    pick = jnp.where(lane == target, 1.0, 0.0).astype(jnp.bfloat16)

    for copy in copies:
        copy.wait()
    total = None
    for first, last in ((0, 4), (4, NPZ)):
        joined = jnp.concatenate(
            [cubes[q].reshape(PATCH * PATCH, PATCH) for q in range(first, last)], axis=1
        )
        high, low = halves(joined)
        rows = pick[PATCH * first : PATCH * last]
        part = dot(high, rows, 0) + dot(low, rows, 0)
        total = part if total is None else total + part
    spectra_ref[...] = total[:, :LANES]
    back[...] = total[:, LANES:]
    row = lax.broadcasted_iota(jnp.int32, (SUB, LANES), 0)
    mirror = (SUB - row) % SUB
    for kx in range(PATCH):
        other = (PATCH - kx) % PATCH
        turned = [
            jnp.take_along_axis(
                back[pl.ds(other * PATCH + SUB * g, SUB), :], mirror, axis=0, mode="promise_in_bounds"
            )
            for g in range(4)
        ]
        for g in range(4):
            rows = pl.ds(kx * PATCH + SUB * g, SUB)
            mirrored = jnp.where(row == 0, turned[(4 - g) % 4], turned[3 - g])
            spectra_ref[rows, :] = spectra_ref[rows, :] + mirrored


def prepare(index, shift, bank, rhs):
    smem = pl.BlockSpec(memory_space=pltpu.SMEM)
    vmem = pl.BlockSpec(memory_space=VMEM)
    return pl.pallas_call(
        prepare_kernel,
        out_shape=[
            jax.ShapeDtypeStruct((PATCH * PATCH, LANES), jnp.float32),
            jax.ShapeDtypeStruct((LANES, 2 * LANES), jnp.float32),
            jax.ShapeDtypeStruct((HALF * HALF, 2 * LANES), jnp.float32),
        ],
        in_specs=[smem, smem, pl.BlockSpec(memory_space=pltpu.HBM), vmem],
        out_specs=[vmem] * 3,
        scratch_shapes=[
            VMEM((NPZ, PATCH, PATCH, PATCH), jnp.float32),
            VMEM((PATCH * PATCH, LANES), jnp.float32),
            pltpu.SemaphoreType.DMA((NPZ,)),
        ],
        compiler_params=pltpu.CompilerParams(vmem_limit_bytes=50 * 2**20),
        cost_estimate=pl.CostEstimate(flops=400_000_000, bytes_accessed=8_000_000, transcendentals=0),
        name="prepare",
    )(index, shift, bank, rhs)


PITCH = 40


def strided(h, y):
    return pl.ds(SUB * PITCH * h + y, SUB, stride=PITCH)


def forward_kernel(window_ref, spectra_ref, own_ref, rhs_ref, damping_ref, b10, b01, b11,
                   real, imag, sums_ref, sums, sem):
    window = halves(window_ref[...])

    for xq, yq, block in ((0, 0, None), (1, 0, b10), (0, 1, b01), (1, 1, b11)):
        if block is None:
            result = own_ref[...]
        else:
            result = dot3(halves(block[...].reshape(HALF * HALF, LANES)), window, 0)
        for i in range(HALF):
            rows = pl.ds((HALF * xq + i) * PITCH + HALF * yq, HALF)
            real[rows, :] = result[HALF * i : HALF * (i + 1), :LANES]
            imag[rows, :] = result[HALF * i : HALF * (i + 1), LANES:]

    for h in range(4):
        out = dft32(lambda y: (real[strided(h, y), :] * TAPER[y], imag[strided(h, y), :] * TAPER[y]), -1)
        for k, (re, im) in enumerate(out):
            real[strided(h, k), :] = re
            imag[strided(h, k), :] = im

    energy = jnp.zeros((SUB, LANES), jnp.float32)
    for g in range(4):
        def rows(x):
            return pl.ds(x * PITCH + SUB * g, SUB)

        out = dft32(lambda x: (real[rows(x), :] * TAPER[x], imag[rows(x), :] * TAPER[x]), -1)
        for k, (re, im) in enumerate(out):
            s = spectra_ref[pl.ds(k * PATCH + SUB * g, SUB), :]
            sre, sim = s * re, s * im
            energy = energy + (sre * re + sim * im)
            real[rows(k), :] = sre
            imag[rows(k), :] = sim

    square = rhs_ref[...] * rhs_ref[...]
    rr = jnp.sum(square)
    dd = jnp.sum(square * damping_ref[...]) + jnp.sum(energy) * (1.0 / PATCH**3)
    lane = lax.broadcasted_iota(jnp.int32, sums.shape, len(sums.shape) - 1)
    sums[...] = jnp.where(lane == 0, rr, jnp.where(lane == 1, dd, 0.0))
    leaving = pltpu.make_async_copy(sums, sums_ref, sem)
    leaving.start()
    leaving.wait()


def forward(window, spectra, own, rhs, damping, blocks, copies):
    vmem = pl.BlockSpec(memory_space=VMEM)
    return pl.pallas_call(
        forward_kernel,
        out_shape=[jax.ShapeDtypeStruct((PATCH * PITCH, LANES), jnp.float32)] * 2
        + [jax.ShapeDtypeStruct((copies, 1, LANES), jnp.float32)],
        in_specs=[vmem] * 8,
        out_specs=[vmem] * 2 + [pl.BlockSpec(memory_space=pltpu.HBM)],
        scratch_shapes=[VMEM((copies, 1, LANES), jnp.float32), pltpu.SemaphoreType.DMA],
        compiler_params=pltpu.CompilerParams(vmem_limit_bytes=32 * 2**20),
        cost_estimate=pl.CostEstimate(flops=800_000_000, bytes_accessed=4_000_000, transcendentals=0),
        name="forward",
    )(window, spectra, own, rhs, damping, *blocks)


def inverse_kernel(window_ref, real, imag, o10, o01, o11, near_ref, back_real, back_imag):
    window = halves(window_ref[...])

    for g in range(4):
        def rows(x):
            return pl.ds(x * PITCH + SUB * g, SUB)

        out = dft32(lambda k: (real[rows(k), :], imag[rows(k), :]), 1)
        for x, (re, im) in enumerate(out):
            back_real[rows(x), :] = re * (TAPER[x] / PATCH**3)
            back_imag[rows(x), :] = im * (TAPER[x] / PATCH**3)

    for h in range(4):
        out = dft32(lambda k: (back_real[strided(h, k), :], back_imag[strided(h, k), :]), 1)
        for y, (re, im) in enumerate(out):
            back_real[strided(h, y), :] = re * TAPER[y]
            back_imag[strided(h, y), :] = im * TAPER[y]

    for xq, yq, out in ((0, 0, near_ref), (1, 1, o11), (0, 1, o01), (1, 0, o10)):
        pieces = []
        for i in range(HALF):
            rows = pl.ds((HALF * xq + i) * PITCH + HALF * yq, HALF)
            pieces.append(jnp.concatenate([back_real[rows, :], back_imag[rows, :]], axis=1))
        both = jnp.concatenate(pieces, axis=0)
        if out is near_ref:
            near_ref[...] = both
        else:
            out[...] = dot3(halves(both), window, 1).reshape(HALF, HALF, LANES)


def inverse(window, real, imag):
    vmem = pl.BlockSpec(memory_space=VMEM)
    return pl.pallas_call(
        inverse_kernel,
        out_shape=[jax.ShapeDtypeStruct((HALF, HALF, LANES), jnp.float32)] * 3
        + [jax.ShapeDtypeStruct((HALF * HALF, 2 * LANES), jnp.float32)],
        in_specs=[vmem] * 3,
        out_specs=[vmem] * 4,
        scratch_shapes=[VMEM((PATCH * PITCH, LANES), jnp.float32)] * 2,
        compiler_params=pltpu.CompilerParams(vmem_limit_bytes=32 * 2**20),
        cost_estimate=pl.CostEstimate(flops=800_000_000, bytes_accessed=4_000_000, transcendentals=0),
        name="inverse",
    )(window, real, imag)


def near_kernel(window_ref, near_ref, rhs_ref, damping_ref, image_ref):
    own = dot3(halves(near_ref[...]), halves(window_ref[...]), 1)
    image_ref[...] = own.reshape(image_ref.shape) + damping_ref[...] * rhs_ref[...]


def near(window, inner, rhs, damping):
    vmem = pl.BlockSpec(memory_space=VMEM)
    return pl.pallas_call(
        near_kernel,
        out_shape=jax.ShapeDtypeStruct(rhs.shape, jnp.float32),
        in_specs=[vmem] * 4,
        out_specs=vmem,
        compiler_params=pltpu.CompilerParams(vmem_limit_bytes=32 * 2**20),
        cost_estimate=pl.CostEstimate(flops=20_000_000, bytes_accessed=1_000_000, transcendentals=0),
        name="near",
    )(window, inner, rhs, damping)


def finish_kernel(sums_ref, others_ref, rhs_ref, own, r11, r01, r10, solution_ref, residual_ref):
    totals = [jnp.sum(ref[...], axis=(0, 1), keepdims=True)[0] for ref in (sums_ref, others_ref)]
    totals = totals[0] + totals[1]
    lane = lax.broadcasted_iota(jnp.int32, totals.shape, 1)
    rr = jnp.sum(jnp.where(lane == 0, totals, 0.0), axis=1, keepdims=True)
    dd = jnp.sum(jnp.where(lane == 1, totals, 0.0), axis=1, keepdims=True)
    alpha = (rr / dd)[None]
    rhs = rhs_ref[...]
    image = (own[...] + r11[...]) + (r01[...] + r10[...])
    solution_ref[...] = alpha * rhs
    residual_ref[...] = rhs - alpha * image


def finish(sums, others, rhs, parts):
    block = jax.ShapeDtypeStruct(rhs.shape, jnp.float32)
    vmem = pl.BlockSpec(memory_space=VMEM)
    return pl.pallas_call(
        finish_kernel,
        out_shape=[block, block],
        in_specs=[vmem] * 7,
        out_specs=[vmem] * 2,
        compiler_params=pltpu.CompilerParams(vmem_limit_bytes=8 * 2**20),
        cost_estimate=pl.CostEstimate(flops=1_000_000, bytes_accessed=1_000_000, transcendentals=0),
        name="finish",
    )(sums, others, rhs, *parts)


def moved(x, by_x, by_y):
    nx, ny = lax.axis_size("gx"), lax.axis_size("gy")
    pairs = [
        (i * ny + j, (i + by_x) * ny + j + by_y)
        for i in range(nx)
        for j in range(ny)
        if 0 <= i + by_x < nx and 0 <= j + by_y < ny
    ]
    return lax.ppermute(x, ("gx", "gy"), pairs)


def body(migrated, prior_sample, damping, psf_bank, psf_index, z_shift):
    rhs = migrated + damping * prior_sample
    nx, ny = lax.axis_size("gx"), lax.axis_size("gy")
    halo = [moved(rhs, -1, 0), moved(rhs, 0, -1), moved(rhs, -1, -1)]
    spectra, window, own = prepare(psf_index, z_shift, psf_bank, rhs)
    real, imag, sums = forward(window, spectra, own, rhs, damping, halo, nx * ny // 2)
    groups = [[i * ny + j for i in range(nx) for j in range(k, ny, 2)] for k in range(2)]
    sums = lax.all_to_all(sums, ("gx", "gy"), 0, 0, axis_index_groups=groups)
    others = lax.ppermute(sums, "gy", [(j, j ^ 1) for j in range(ny)])
    o10, o01, o11, inner = inverse(window, real, imag)
    back = [moved(o11, 1, 1), moved(o01, 0, 1), moved(o10, 1, 0)]
    image = near(window, inner, rhs, damping)
    return tuple(finish(sums, others, rhs, [image] + back))


def solution(mesh):
    block = P("gx", "gy", None)
    return jax.shard_map(
        body,
        mesh=mesh,
        in_specs=(block, block, block, P(), block, P("gx", "gy")),
        out_specs=(block, block),
        check_vma=False,
    )
```

```python
import math

import jax
import jax.numpy as jnp
from jax import lax
from jax.experimental import pallas as pl
from jax.experimental.pallas import tpu as pltpu
from jax.sharding import PartitionSpec as P

PATCH = 32
HALF = 16
NPZ = 6
KZ = 17
LANES = 128
SUB = 8
VMEM = pltpu.VMEM


TAPER = [math.sin(math.pi * (i + 0.5) / PATCH) for i in range(PATCH)]


def twiddle(value, k, n, sign):
    k %= n
    re, im = value
    if k == 0:
        return value
    if 4 * k == n:
        return (-im, re) if sign > 0 else (im, -re)
    if 2 * k == n:
        return (-re, -im)
    if 4 * k == 3 * n:
        return (im, -re) if sign > 0 else (-im, re)
    c = math.cos(2.0 * math.pi * k / n)
    s = sign * math.sin(2.0 * math.pi * k / n)
    if 8 * k % n == 0:
        h = abs(c)
        cs, ss = (1 if c > 0 else -1), (1 if s > 0 else -1)
        if cs == ss:
            a, b = re - im, re + im
            return (a * (h * cs), b * (h * cs))
        a, b = re + im, im - re
        return (a * (h * cs), b * (h * cs))
    return (re * c - im * s, re * s + im * c)


def add(a, b):
    return (a[0] + b[0], a[1] + b[1])


def sub(a, b):
    return (a[0] - b[0], a[1] - b[1])


def dft4(x, sign):
    a, b = add(x[0], x[2]), sub(x[0], x[2])
    c, d = add(x[1], x[3]), twiddle(sub(x[1], x[3]), 1, 4, sign)
    return [add(a, c), add(b, d), sub(a, c), sub(b, d)]


def dft8(x, sign):
    even = dft4(x[0::2], sign)
    odd = [twiddle(v, k, 8, sign) for k, v in enumerate(dft4(x[1::2], sign))]
    return [add(even[k], odd[k]) for k in range(4)] + [sub(even[k], odd[k]) for k in range(4)]


def dft32(load, sign):
    first = []
    for n2 in range(8):
        part = dft4([load(8 * n1 + n2) for n1 in range(4)], sign)
        first.append([twiddle(v, n2 * k1, 32, sign) for k1, v in enumerate(part)])
    out = [None] * 32
    for k1 in range(4):
        part = dft8([first[n2][k1] for n2 in range(8)], sign)
        for k2 in range(8):
            out[k1 + 4 * k2] = part[k2]
    return out


def halves(value):
    high = value.astype(jnp.bfloat16)
    return high, (value - high.astype(jnp.float32)).astype(jnp.bfloat16)


def dot(a, b, contract_b):
    return lax.dot_general(a, b, (((1,), (contract_b,)), ((), ())), preferred_element_type=jnp.float32)


def dot3(a, b, contract_b):
    return dot(a[0], b[0], contract_b) + (dot(a[1], b[0], contract_b) + dot(a[0], b[1], contract_b))


def lookup(values, places):
    lane = lax.broadcasted_iota(jnp.int32, (SUB, LANES), 1)
    table = jnp.zeros((SUB, LANES), jnp.float32)
    for i, value in enumerate(values):
        table = jnp.where(lane == i, value, table)
    return jnp.take_along_axis(table, places, axis=1, mode="promise_in_bounds")


COSINES = [math.cos(2.0 * math.pi * i / PATCH) for i in range(PATCH)]
COSINES[8] = COSINES[24] = 0.0


def window_of(shift, window_ref):
    lane = lax.broadcasted_iota(jnp.int32, (SUB, LANES), 1)
    p = jnp.zeros_like(lane)
    for q in range(1, NPZ):
        p = jnp.where(lane >= KZ * q, q, p)
    kz = lane - KZ * p
    first = lax.broadcasted_iota(jnp.int32, (SUB, LANES), 0) - shift - HALF * p
    for g in range(LANES // SUB):
        cell = first + SUB * g
        inside = (cell >= 0) & (cell < PATCH) & (lane < KZ * NPZ)
        cell = cell & (PATCH - 1)
        taper = jnp.where(inside, lookup(TAPER, cell), 0.0)
        phase = (kz * cell) & (PATCH - 1)
        rows = pl.ds(SUB * g, SUB)
        window_ref[rows, :LANES] = taper * lookup(COSINES, phase)
        sine = taper * lookup(COSINES, (phase + PATCH // 4) & (PATCH - 1))
        window_ref[rows, LANES:] = jnp.where((kz == 0) | (kz == HALF), 0.0, sine)


def prepare_kernel(index_ref, shift_ref, bank_ref, block_ref,
                   spectra_ref, window_ref, own_ref, cubes, back, sems):
    copies = [
        pltpu.make_async_copy(bank_ref.at[index_ref[0, 0, p]], cubes.at[p], sems.at[p]) for p in range(NPZ)
    ]
    for copy in copies:
        copy.start()

    window_of(shift_ref[0, 0], window_ref)
    own_ref[...] = dot3(halves(block_ref[...].reshape(HALF * HALF, LANES)), halves(window_ref[...]), 0)

    source = lax.broadcasted_iota(jnp.int32, (NPZ * PATCH, 2 * LANES), 0)
    lane = lax.broadcasted_iota(jnp.int32, (NPZ * PATCH, 2 * LANES), 1)
    p, kz = source // PATCH, source % PATCH
    target = jnp.where(kz < KZ, KZ * p + kz, LANES + KZ * p + PATCH - kz)
    pick = jnp.where(lane == target, 1.0, 0.0).astype(jnp.bfloat16)

    for copy in copies:
        copy.wait()
    total = None
    for first, last in ((0, 4), (4, NPZ)):
        joined = jnp.concatenate(
            [cubes[q].reshape(PATCH * PATCH, PATCH) for q in range(first, last)], axis=1
        )
        high, low = halves(joined)
        rows = pick[PATCH * first : PATCH * last]
        part = dot(high, rows, 0) + dot(low, rows, 0)
        total = part if total is None else total + part
    spectra_ref[...] = total[:, :LANES]
    back[...] = total[:, LANES:]
    row = lax.broadcasted_iota(jnp.int32, (SUB, LANES), 0)
    mirror = (SUB - row) % SUB
    for kx in range(PATCH):
        other = (PATCH - kx) % PATCH
        turned = [
            jnp.take_along_axis(
                back[pl.ds(other * PATCH + SUB * g, SUB), :], mirror, axis=0, mode="promise_in_bounds"
            )
            for g in range(4)
        ]
        for g in range(4):
            rows = pl.ds(kx * PATCH + SUB * g, SUB)
            mirrored = jnp.where(row == 0, turned[(4 - g) % 4], turned[3 - g])
            spectra_ref[rows, :] = spectra_ref[rows, :] + mirrored


def prepare(index, shift, bank, rhs):
    smem = pl.BlockSpec(memory_space=pltpu.SMEM)
    vmem = pl.BlockSpec(memory_space=VMEM)
    return pl.pallas_call(
        prepare_kernel,
        out_shape=[
            jax.ShapeDtypeStruct((PATCH * PATCH, LANES), jnp.float32),
            jax.ShapeDtypeStruct((LANES, 2 * LANES), jnp.float32),
            jax.ShapeDtypeStruct((HALF * HALF, 2 * LANES), jnp.float32),
        ],
        in_specs=[smem, smem, pl.BlockSpec(memory_space=pltpu.HBM), vmem],
        out_specs=[vmem] * 3,
        scratch_shapes=[
            VMEM((NPZ, PATCH, PATCH, PATCH), jnp.float32),
            VMEM((PATCH * PATCH, LANES), jnp.float32),
            pltpu.SemaphoreType.DMA((NPZ,)),
        ],
        compiler_params=pltpu.CompilerParams(vmem_limit_bytes=50 * 2**20),
        cost_estimate=pl.CostEstimate(flops=400_000_000, bytes_accessed=8_000_000, transcendentals=0),
        name="prepare",
    )(index, shift, bank, rhs)


PITCH = 40


def patches_kernel(window_ref, spectra_ref, own_ref, rhs_ref, damping_ref, b10, b01, b11,
                   upper, inner, sums_ref, real, imag, held, sums, sem):
    window = halves(window_ref[...])

    for xq, yq, block in ((0, 0, None), (1, 0, b10), (0, 1, b01), (1, 1, b11)):
        if block is None:
            result = own_ref[...]
        else:
            result = dot3(halves(block[...].reshape(HALF * HALF, LANES)), window, 0)
        for i in range(HALF):
            rows = pl.ds((HALF * xq + i) * PITCH + HALF * yq, HALF)
            real[rows, :] = result[HALF * i : HALF * (i + 1), :LANES]
            imag[rows, :] = result[HALF * i : HALF * (i + 1), LANES:]

    def strided(h, y):
        return pl.ds(SUB * PITCH * h + y, SUB, stride=PITCH)

    for h in range(4):
        out = dft32(lambda y: (real[strided(h, y), :] * TAPER[y], imag[strided(h, y), :] * TAPER[y]), -1)
        for k, (re, im) in enumerate(out):
            real[strided(h, k), :] = re
            imag[strided(h, k), :] = im

    energy = jnp.zeros((SUB, LANES), jnp.float32)
    for g in range(4):
        def rows(x):
            return pl.ds(x * PITCH + SUB * g, SUB)

        out = dft32(lambda x: (real[rows(x), :] * TAPER[x], imag[rows(x), :] * TAPER[x]), -1)
        scaled = []
        for k, (re, im) in enumerate(out):
            s = spectra_ref[pl.ds(k * PATCH + SUB * g, SUB), :]
            sre, sim = s * re, s * im
            energy = energy + (sre * re + sim * im)
            scaled.append((sre, sim))
        out = dft32(lambda k: scaled[k], 1)
        for x, (re, im) in enumerate(out):
            real[rows(x), :] = re * (TAPER[x] / PATCH**3)
            imag[rows(x), :] = im * (TAPER[x] / PATCH**3)

    square = rhs_ref[...] * rhs_ref[...]
    rr = jnp.sum(square)
    dd = jnp.sum(square * damping_ref[...]) + jnp.sum(energy) * (1.0 / PATCH**3)
    lane = lax.broadcasted_iota(jnp.int32, sums.shape, len(sums.shape) - 1)
    sums[...] = jnp.where(lane == 0, rr, jnp.where(lane == 1, dd, 0.0))
    leaving = pltpu.make_async_copy(sums, sums_ref, sem)
    leaving.start()

    for h in range(4):
        out = dft32(lambda k: (real[strided(h, k), :], imag[strided(h, k), :]), 1)
        for y, (re, im) in enumerate(out):
            real[strided(h, y), :] = re * TAPER[y]
            imag[strided(h, y), :] = im * TAPER[y]

    for xq in range(2):
        for i in range(HALF):
            rows = pl.ds((HALF * xq + i) * PITCH, PATCH)
            target = pl.ds(i * PATCH, PATCH)
            both = jnp.concatenate([real[rows, :], imag[rows, :]], axis=1)
            if xq == 0:
                inner[target, :] = both
            else:
                held[target, :] = both
    upper[...] = dot3(halves(held[...]), window, 1).reshape(upper.shape)
    leaving.wait()


def patches(window, spectra, own, rhs, damping, blocks, copies):
    vmem = pl.BlockSpec(memory_space=VMEM)
    return pl.pallas_call(
        patches_kernel,
        out_shape=[jax.ShapeDtypeStruct((HALF, PATCH, LANES), jnp.float32)]
        + [jax.ShapeDtypeStruct((HALF * PATCH, 2 * LANES), jnp.float32), jax.ShapeDtypeStruct((copies, 1, LANES), jnp.float32)],
        in_specs=[vmem] * 8,
        out_specs=[vmem] * 2 + [pl.BlockSpec(memory_space=pltpu.HBM)],
        scratch_shapes=[VMEM((PATCH * PITCH, LANES), jnp.float32)] * 2
        + [
            VMEM((HALF * PATCH, 2 * LANES), jnp.float32),
            VMEM((copies, 1, LANES), jnp.float32),
            pltpu.SemaphoreType.DMA,
        ],
        compiler_params=pltpu.CompilerParams(vmem_limit_bytes=32 * 2**20),
        cost_estimate=pl.CostEstimate(flops=800_000_000, bytes_accessed=4_000_000, transcendentals=0),
        name="patches",
    )(window, spectra, own, rhs, damping, *blocks)


def near_kernel(window_ref, inner, rhs_ref, damping_ref, arrived, image_ref, leaving_ref):
    lower = dot3(halves(inner[...]), halves(window_ref[...]), 1).reshape(arrived.shape) + arrived[...]
    image_ref[...] = lower[:, :HALF] + damping_ref[...] * rhs_ref[...]
    leaving_ref[...] = lower[:, HALF:]


def near(window, inner, rhs, damping, arrived):
    vmem = pl.BlockSpec(memory_space=VMEM)
    return pl.pallas_call(
        near_kernel,
        out_shape=[jax.ShapeDtypeStruct(rhs.shape, jnp.float32)] * 2,
        in_specs=[vmem] * 5,
        out_specs=[vmem] * 2,
        compiler_params=pltpu.CompilerParams(vmem_limit_bytes=32 * 2**20),
        cost_estimate=pl.CostEstimate(flops=20_000_000, bytes_accessed=1_000_000, transcendentals=0),
        name="near",
    )(window, inner, rhs, damping, arrived)


def finish_kernel(sums_ref, others_ref, rhs_ref, own, from_y, solution_ref, residual_ref):
    totals = [jnp.sum(ref[...], axis=(0, 1), keepdims=True)[0] for ref in (sums_ref, others_ref)]
    totals = totals[0] + totals[1]
    lane = lax.broadcasted_iota(jnp.int32, totals.shape, 1)
    rr = jnp.sum(jnp.where(lane == 0, totals, 0.0), axis=1, keepdims=True)
    dd = jnp.sum(jnp.where(lane == 1, totals, 0.0), axis=1, keepdims=True)
    alpha = (rr / dd)[None]
    rhs = rhs_ref[...]
    image = own[...] + from_y[...]
    solution_ref[...] = alpha * rhs
    residual_ref[...] = rhs - alpha * image


def finish(sums, others, rhs, parts):
    block = jax.ShapeDtypeStruct(rhs.shape, jnp.float32)
    vmem = pl.BlockSpec(memory_space=VMEM)
    return pl.pallas_call(
        finish_kernel,
        out_shape=[block, block],
        in_specs=[vmem] * 5,
        out_specs=[vmem] * 2,
        compiler_params=pltpu.CompilerParams(vmem_limit_bytes=8 * 2**20),
        cost_estimate=pl.CostEstimate(flops=1_000_000, bytes_accessed=1_000_000, transcendentals=0),
        name="finish",
    )(sums, others, rhs, *parts)


def moved(x, by_x, by_y):
    nx, ny = lax.axis_size("gx"), lax.axis_size("gy")
    pairs = [
        (i * ny + j, (i + by_x) * ny + j + by_y)
        for i in range(nx)
        for j in range(ny)
        if 0 <= i + by_x < nx and 0 <= j + by_y < ny
    ]
    return lax.ppermute(x, ("gx", "gy"), pairs)


def body(migrated, prior_sample, damping, psf_bank, psf_index, z_shift):
    rhs = migrated + damping * prior_sample
    nx, ny = lax.axis_size("gx"), lax.axis_size("gy")
    halo = [moved(rhs, -1, 0), moved(rhs, 0, -1), moved(rhs, -1, -1)]
    spectra, window, own = prepare(psf_index, z_shift, psf_bank, rhs)
    upper, inner, sums = patches(window, spectra, own, rhs, damping, halo, nx * ny // 2)
    from_x = moved(upper, 1, 0)
    groups = [[i * ny + j for i in range(nx) for j in range(k, ny, 2)] for k in range(2)]
    sums = lax.all_to_all(sums, ("gx", "gy"), 0, 0, axis_index_groups=groups)
    others = lax.ppermute(sums, "gy", [(j, j ^ 1) for j in range(ny)])
    image, leaving = near(window, inner, rhs, damping, from_x)
    from_y = moved(leaving, 0, 1)
    return tuple(finish(sums, others, rhs, [image, from_y]))


def solution(mesh):
    block = P("gx", "gy", None)
    return jax.shard_map(
        body,
        mesh=mesh,
        in_specs=(block, block, block, P(), block, P("gx", "gy")),
        out_specs=(block, block),
        check_vma=False,
    )
```

```python
import math

import jax
import jax.numpy as jnp
from jax import lax
from jax.experimental import pallas as pl
from jax.experimental.pallas import tpu as pltpu
from jax.sharding import PartitionSpec as P

PATCH = 32
HALF = 16
NPZ = 6
KZ = 17
LANES = 128
SUB = 8
VMEM = pltpu.VMEM


TAPER = [math.sin(math.pi * (i + 0.5) / PATCH) for i in range(PATCH)]


def twiddle(value, k, n, sign):
    k %= n
    re, im = value
    if k == 0:
        return value
    if 4 * k == n:
        return (-im, re) if sign > 0 else (im, -re)
    if 2 * k == n:
        return (-re, -im)
    if 4 * k == 3 * n:
        return (im, -re) if sign > 0 else (-im, re)
    c = math.cos(2.0 * math.pi * k / n)
    s = sign * math.sin(2.0 * math.pi * k / n)
    if 8 * k % n == 0:
        h = abs(c)
        cs, ss = (1 if c > 0 else -1), (1 if s > 0 else -1)
        if cs == ss:
            a, b = re - im, re + im
            return (a * (h * cs), b * (h * cs))
        a, b = re + im, im - re
        return (a * (h * cs), b * (h * cs))
    return (re * c - im * s, re * s + im * c)


def add(a, b):
    return (a[0] + b[0], a[1] + b[1])


def sub(a, b):
    return (a[0] - b[0], a[1] - b[1])


def dft4(x, sign):
    a, b = add(x[0], x[2]), sub(x[0], x[2])
    c, d = add(x[1], x[3]), twiddle(sub(x[1], x[3]), 1, 4, sign)
    return [add(a, c), add(b, d), sub(a, c), sub(b, d)]


def dft8(x, sign):
    even = dft4(x[0::2], sign)
    odd = [twiddle(v, k, 8, sign) for k, v in enumerate(dft4(x[1::2], sign))]
    return [add(even[k], odd[k]) for k in range(4)] + [sub(even[k], odd[k]) for k in range(4)]


def dft32(load, sign):
    first = []
    for n2 in range(8):
        part = dft4([load(8 * n1 + n2) for n1 in range(4)], sign)
        first.append([twiddle(v, n2 * k1, 32, sign) for k1, v in enumerate(part)])
    out = [None] * 32
    for k1 in range(4):
        part = dft8([first[n2][k1] for n2 in range(8)], sign)
        for k2 in range(8):
            out[k1 + 4 * k2] = part[k2]
    return out


def halves(value):
    high = value.astype(jnp.bfloat16)
    return high, (value - high.astype(jnp.float32)).astype(jnp.bfloat16)


def dot(a, b, contract_b):
    return lax.dot_general(a, b, (((1,), (contract_b,)), ((), ())), preferred_element_type=jnp.float32)


def dot3(a, b, contract_b):
    return dot(a[0], b[0], contract_b) + (dot(a[1], b[0], contract_b) + dot(a[0], b[1], contract_b))


def lookup(values, places):
    lane = lax.broadcasted_iota(jnp.int32, (SUB, LANES), 1)
    table = jnp.zeros((SUB, LANES), jnp.float32)
    for i, value in enumerate(values):
        table = jnp.where(lane == i, value, table)
    return jnp.take_along_axis(table, places, axis=1, mode="promise_in_bounds")


COSINES = [math.cos(2.0 * math.pi * i / PATCH) for i in range(PATCH)]
COSINES[8] = COSINES[24] = 0.0


def window_of(shift, window_ref):
    lane = lax.broadcasted_iota(jnp.int32, (SUB, LANES), 1)
    p = jnp.zeros_like(lane)
    for q in range(1, NPZ):
        p = jnp.where(lane >= KZ * q, q, p)
    kz = lane - KZ * p
    first = lax.broadcasted_iota(jnp.int32, (SUB, LANES), 0) - shift - HALF * p
    for g in range(LANES // SUB):
        cell = first + SUB * g
        inside = (cell >= 0) & (cell < PATCH) & (lane < KZ * NPZ)
        cell = cell & (PATCH - 1)
        taper = jnp.where(inside, lookup(TAPER, cell), 0.0)
        phase = (kz * cell) & (PATCH - 1)
        rows = pl.ds(SUB * g, SUB)
        window_ref[rows, :LANES] = taper * lookup(COSINES, phase)
        sine = taper * lookup(COSINES, (phase + PATCH // 4) & (PATCH - 1))
        window_ref[rows, LANES:] = jnp.where((kz == 0) | (kz == HALF), 0.0, sine)


def prepare_kernel(index_ref, shift_ref, bank_ref, block_ref,
                   spectra_ref, window_ref, own_ref, cubes, back, sems):
    copies = [
        pltpu.make_async_copy(bank_ref.at[index_ref[0, 0, p]], cubes.at[p], sems.at[p]) for p in range(NPZ)
    ]
    for copy in copies:
        copy.start()

    window_of(shift_ref[0, 0], window_ref)
    own_ref[...] = dot3(halves(block_ref[...].reshape(HALF * HALF, LANES)), halves(window_ref[...]), 0)

    source = lax.broadcasted_iota(jnp.int32, (NPZ * PATCH, 2 * LANES), 0)
    lane = lax.broadcasted_iota(jnp.int32, (NPZ * PATCH, 2 * LANES), 1)
    p, kz = source // PATCH, source % PATCH
    target = jnp.where(kz < KZ, KZ * p + kz, LANES + KZ * p + PATCH - kz)
    pick = jnp.where(lane == target, 1.0, 0.0).astype(jnp.bfloat16)

    for copy in copies:
        copy.wait()
    total = None
    for first, last in ((0, 4), (4, NPZ)):
        joined = jnp.concatenate(
            [cubes[q].reshape(PATCH * PATCH, PATCH) for q in range(first, last)], axis=1
        )
        high, low = halves(joined)
        rows = pick[PATCH * first : PATCH * last]
        part = dot(high, rows, 0) + dot(low, rows, 0)
        total = part if total is None else total + part
    spectra_ref[...] = total[:, :LANES]
    back[...] = total[:, LANES:]
    row = lax.broadcasted_iota(jnp.int32, (SUB, LANES), 0)
    mirror = (SUB - row) % SUB
    for kx in range(PATCH):
        other = (PATCH - kx) % PATCH
        turned = [
            jnp.take_along_axis(
                back[pl.ds(other * PATCH + SUB * g, SUB), :], mirror, axis=0, mode="promise_in_bounds"
            )
            for g in range(4)
        ]
        for g in range(4):
            rows = pl.ds(kx * PATCH + SUB * g, SUB)
            mirrored = jnp.where(row == 0, turned[(4 - g) % 4], turned[3 - g])
            spectra_ref[rows, :] = spectra_ref[rows, :] + mirrored


def prepare(index, shift, bank, rhs):
    smem = pl.BlockSpec(memory_space=pltpu.SMEM)
    vmem = pl.BlockSpec(memory_space=VMEM)
    return pl.pallas_call(
        prepare_kernel,
        out_shape=[
            jax.ShapeDtypeStruct((PATCH * PATCH, LANES), jnp.float32),
            jax.ShapeDtypeStruct((LANES, 2 * LANES), jnp.float32),
            jax.ShapeDtypeStruct((HALF * HALF, 2 * LANES), jnp.float32),
        ],
        in_specs=[smem, smem, pl.BlockSpec(memory_space=pltpu.HBM), vmem],
        out_specs=[vmem] * 3,
        scratch_shapes=[
            VMEM((NPZ, PATCH, PATCH, PATCH), jnp.float32),
            VMEM((PATCH * PATCH, LANES), jnp.float32),
            pltpu.SemaphoreType.DMA((NPZ,)),
        ],
        compiler_params=pltpu.CompilerParams(vmem_limit_bytes=50 * 2**20),
        cost_estimate=pl.CostEstimate(flops=400_000_000, bytes_accessed=8_000_000, transcendentals=0),
        name="prepare",
    )(index, shift, bank, rhs)


PITCH = 40


def strided(h, y):
    return pl.ds(SUB * PITCH * h + y, SUB, stride=PITCH)


def patches_kernel(window_ref, spectra_ref, own_ref, rhs_ref, damping_ref, b10, b11, b01,
                   upper, real, imag, sums_ref, held, sums, sem):
    window = halves(window_ref[...])

    for xq, yq, block in ((0, 0, None), (1, 0, b10), (0, 1, b01), (1, 1, b11)):
        if block is None:
            result = own_ref[...]
        else:
            result = dot3(halves(block[...].reshape(HALF * HALF, LANES)), window, 0)
        for i in range(HALF):
            rows = pl.ds((HALF * xq + i) * PITCH + HALF * yq, HALF)
            real[rows, :] = result[HALF * i : HALF * (i + 1), :LANES]
            imag[rows, :] = result[HALF * i : HALF * (i + 1), LANES:]

    for h in range(4):
        out = dft32(lambda y: (real[strided(h, y), :] * TAPER[y], imag[strided(h, y), :] * TAPER[y]), -1)
        for k, (re, im) in enumerate(out):
            real[strided(h, k), :] = re
            imag[strided(h, k), :] = im

    energy = jnp.zeros((SUB, LANES), jnp.float32)
    for g in range(4):
        def rows(x):
            return pl.ds(x * PITCH + SUB * g, SUB)

        out = dft32(lambda x: (real[rows(x), :] * TAPER[x], imag[rows(x), :] * TAPER[x]), -1)
        scaled = []
        for k, (re, im) in enumerate(out):
            s = spectra_ref[pl.ds(k * PATCH + SUB * g, SUB), :]
            sre, sim = s * re, s * im
            energy = energy + (sre * re + sim * im)
            scaled.append((sre, sim))
        out = dft32(lambda k: scaled[k], 1)
        for x, (re, im) in enumerate(out):
            real[rows(x), :] = re * (TAPER[x] / PATCH**3)
            imag[rows(x), :] = im * (TAPER[x] / PATCH**3)

    square = rhs_ref[...] * rhs_ref[...]
    rr = jnp.sum(square)
    dd = jnp.sum(square * damping_ref[...]) + jnp.sum(energy) * (1.0 / PATCH**3)
    lane = lax.broadcasted_iota(jnp.int32, sums.shape, len(sums.shape) - 1)
    sums[...] = jnp.where(lane == 0, rr, jnp.where(lane == 1, dd, 0.0))
    leaving = pltpu.make_async_copy(sums, sums_ref, sem)
    leaving.start()

    for h in range(2, 4):
        out = dft32(lambda k: (real[strided(h, k), :], imag[strided(h, k), :]), 1)
        for y, (re, im) in enumerate(out):
            real[strided(h, y), :] = re * TAPER[y]
            imag[strided(h, y), :] = im * TAPER[y]
    for i in range(HALF):
        rows = pl.ds((HALF + i) * PITCH, PATCH)
        held[pl.ds(i * PATCH, PATCH), :] = jnp.concatenate([real[rows, :], imag[rows, :]], axis=1)
    upper[...] = dot3(halves(held[...]), window, 1).reshape(upper.shape)
    leaving.wait()


def patches(window, spectra, own, rhs, damping, blocks, copies):
    vmem = pl.BlockSpec(memory_space=VMEM)
    return pl.pallas_call(
        patches_kernel,
        out_shape=[jax.ShapeDtypeStruct((HALF, PATCH, LANES), jnp.float32)]
        + [jax.ShapeDtypeStruct((PATCH * PITCH, LANES), jnp.float32)] * 2
        + [jax.ShapeDtypeStruct((copies, 1, LANES), jnp.float32)],
        in_specs=[vmem] * 8,
        out_specs=[vmem] * 3 + [pl.BlockSpec(memory_space=pltpu.HBM)],
        scratch_shapes=[
            VMEM((HALF * PATCH, 2 * LANES), jnp.float32),
            VMEM((copies, 1, LANES), jnp.float32),
            pltpu.SemaphoreType.DMA,
        ],
        compiler_params=pltpu.CompilerParams(vmem_limit_bytes=32 * 2**20),
        cost_estimate=pl.CostEstimate(flops=800_000_000, bytes_accessed=4_000_000, transcendentals=0),
        name="patches",
    )(window, spectra, own, rhs, damping, *blocks)


def near_kernel(window_ref, real, imag, rhs_ref, damping_ref, arrived, image_ref, leaving_ref, held):
    for h in range(2):
        out = dft32(lambda k: (real[strided(h, k), :], imag[strided(h, k), :]), 1)
        for y, (re, im) in enumerate(out):
            held[0, strided(h, y), :] = re * TAPER[y]
            held[1, strided(h, y), :] = im * TAPER[y]
    both = [
        jnp.concatenate([held[part, pl.ds(i * PITCH, PATCH), :] for i in range(HALF)], axis=0)
        for part in range(2)
    ]
    both = jnp.concatenate(both, axis=1)
    lower = dot3(halves(both), halves(window_ref[...]), 1).reshape(arrived.shape) + arrived[...]
    image_ref[...] = lower[:, :HALF] + damping_ref[...] * rhs_ref[...]
    leaving_ref[...] = lower[:, HALF:]


def near(window, real, imag, rhs, damping, arrived):
    vmem = pl.BlockSpec(memory_space=VMEM)
    return pl.pallas_call(
        near_kernel,
        out_shape=[jax.ShapeDtypeStruct(rhs.shape, jnp.float32)] * 2,
        in_specs=[vmem] * 6,
        out_specs=[vmem] * 2,
        scratch_shapes=[VMEM((2, HALF * PITCH, LANES), jnp.float32)],
        compiler_params=pltpu.CompilerParams(vmem_limit_bytes=32 * 2**20),
        cost_estimate=pl.CostEstimate(flops=20_000_000, bytes_accessed=1_000_000, transcendentals=0),
        name="near",
    )(window, real, imag, rhs, damping, arrived)


def finish_kernel(sums_ref, others_ref, rhs_ref, own, from_y, solution_ref, residual_ref):
    totals = [jnp.sum(ref[...], axis=(0, 1), keepdims=True)[0] for ref in (sums_ref, others_ref)]
    totals = totals[0] + totals[1]
    lane = lax.broadcasted_iota(jnp.int32, totals.shape, 1)
    rr = jnp.sum(jnp.where(lane == 0, totals, 0.0), axis=1, keepdims=True)
    dd = jnp.sum(jnp.where(lane == 1, totals, 0.0), axis=1, keepdims=True)
    alpha = (rr / dd)[None]
    rhs = rhs_ref[...]
    image = own[...] + from_y[...]
    solution_ref[...] = alpha * rhs
    residual_ref[...] = rhs - alpha * image


def finish(sums, others, rhs, parts):
    block = jax.ShapeDtypeStruct(rhs.shape, jnp.float32)
    vmem = pl.BlockSpec(memory_space=VMEM)
    return pl.pallas_call(
        finish_kernel,
        out_shape=[block, block],
        in_specs=[vmem] * 5,
        out_specs=[vmem] * 2,
        compiler_params=pltpu.CompilerParams(vmem_limit_bytes=8 * 2**20),
        cost_estimate=pl.CostEstimate(flops=1_000_000, bytes_accessed=1_000_000, transcendentals=0),
        name="finish",
    )(sums, others, rhs, *parts)


def moved(x, by_x, by_y):
    nx, ny = lax.axis_size("gx"), lax.axis_size("gy")
    pairs = [
        (i * ny + j, (i + by_x) * ny + j + by_y)
        for i in range(nx)
        for j in range(ny)
        if 0 <= i + by_x < nx and 0 <= j + by_y < ny
    ]
    return lax.ppermute(x, ("gx", "gy"), pairs)


def body(migrated, prior_sample, damping, psf_bank, psf_index, z_shift):
    rhs = migrated + damping * prior_sample
    nx, ny = lax.axis_size("gx"), lax.axis_size("gy")
    from_x, from_xy, from_y = moved(rhs, -1, 0), moved(rhs, -1, -1), moved(rhs, 0, -1)
    spectra, window, own = prepare(psf_index, z_shift, psf_bank, rhs)
    upper, real, imag, sums = patches(
        window, spectra, own, rhs, damping, [from_x, from_xy, from_y], nx * ny // 2
    )
    from_x = moved(upper, 1, 0)
    groups = [[i * ny + j for i in range(nx) for j in range(k, ny, 2)] for k in range(2)]
    sums = lax.all_to_all(sums, ("gx", "gy"), 0, 0, axis_index_groups=groups)
    others = lax.ppermute(sums, "gy", [(j, j ^ 1) for j in range(ny)])
    image, leaving = near(window, real, imag, rhs, damping, from_x)
    from_y = moved(leaving, 0, 1)
    return tuple(finish(sums, others, rhs, [image, from_y]))


def solution(mesh):
    block = P("gx", "gy", None)
    return jax.shard_map(
        body,
        mesh=mesh,
        in_specs=(block, block, block, P(), block, P("gx", "gy")),
        out_specs=(block, block),
        check_vma=False,
    )
```

```python
import math

import jax
import jax.numpy as jnp
from jax import lax
from jax.experimental import pallas as pl
from jax.experimental.pallas import tpu as pltpu
from jax.sharding import PartitionSpec as P

PATCH = 32
HALF = 16
NPZ = 6
KZ = 17
LANES = 128
SUB = 8
VMEM = pltpu.VMEM


TAPER = [math.sin(math.pi * (i + 0.5) / PATCH) for i in range(PATCH)]


def twiddle(value, k, n, sign):
    k %= n
    re, im = value
    if k == 0:
        return value
    if 4 * k == n:
        return (-im, re) if sign > 0 else (im, -re)
    if 2 * k == n:
        return (-re, -im)
    if 4 * k == 3 * n:
        return (im, -re) if sign > 0 else (-im, re)
    c = math.cos(2.0 * math.pi * k / n)
    s = sign * math.sin(2.0 * math.pi * k / n)
    if 8 * k % n == 0:
        h = abs(c)
        cs, ss = (1 if c > 0 else -1), (1 if s > 0 else -1)
        if cs == ss:
            a, b = re - im, re + im
            return (a * (h * cs), b * (h * cs))
        a, b = re + im, im - re
        return (a * (h * cs), b * (h * cs))
    return (re * c - im * s, re * s + im * c)


def add(a, b):
    return (a[0] + b[0], a[1] + b[1])


def sub(a, b):
    return (a[0] - b[0], a[1] - b[1])


def dft4(x, sign):
    a, b = add(x[0], x[2]), sub(x[0], x[2])
    c, d = add(x[1], x[3]), twiddle(sub(x[1], x[3]), 1, 4, sign)
    return [add(a, c), add(b, d), sub(a, c), sub(b, d)]


def dft8(x, sign):
    even = dft4(x[0::2], sign)
    odd = [twiddle(v, k, 8, sign) for k, v in enumerate(dft4(x[1::2], sign))]
    return [add(even[k], odd[k]) for k in range(4)] + [sub(even[k], odd[k]) for k in range(4)]


def dft32(load, sign):
    first = []
    for n2 in range(8):
        part = dft4([load(8 * n1 + n2) for n1 in range(4)], sign)
        first.append([twiddle(v, n2 * k1, 32, sign) for k1, v in enumerate(part)])
    out = [None] * 32
    for k1 in range(4):
        part = dft8([first[n2][k1] for n2 in range(8)], sign)
        for k2 in range(8):
            out[k1 + 4 * k2] = part[k2]
    return out


def halves(value):
    high = value.astype(jnp.bfloat16)
    return high, (value - high.astype(jnp.float32)).astype(jnp.bfloat16)


def dot(a, b, contract_b):
    return lax.dot_general(a, b, (((1,), (contract_b,)), ((), ())), preferred_element_type=jnp.float32)


def dot3(a, b, contract_b):
    return dot(a[0], b[0], contract_b) + (dot(a[1], b[0], contract_b) + dot(a[0], b[1], contract_b))


def lookup(values, places):
    lane = lax.broadcasted_iota(jnp.int32, (SUB, LANES), 1)
    table = jnp.zeros((SUB, LANES), jnp.float32)
    for i, value in enumerate(values):
        table = jnp.where(lane == i, value, table)
    return jnp.take_along_axis(table, places, axis=1, mode="promise_in_bounds")


COSINES = [math.cos(2.0 * math.pi * i / PATCH) for i in range(PATCH)]
COSINES[8] = COSINES[24] = 0.0


def window_of(shift, window_ref):
    lane = lax.broadcasted_iota(jnp.int32, (SUB, LANES), 1)
    p = jnp.zeros_like(lane)
    for q in range(1, NPZ):
        p = jnp.where(lane >= KZ * q, q, p)
    kz = lane - KZ * p
    first = lax.broadcasted_iota(jnp.int32, (SUB, LANES), 0) - shift - HALF * p
    for g in range(LANES // SUB):
        cell = first + SUB * g
        inside = (cell >= 0) & (cell < PATCH) & (lane < KZ * NPZ)
        cell = cell & (PATCH - 1)
        taper = jnp.where(inside, lookup(TAPER, cell), 0.0)
        phase = (kz * cell) & (PATCH - 1)
        rows = pl.ds(SUB * g, SUB)
        window_ref[rows, :LANES] = taper * lookup(COSINES, phase)
        sine = taper * lookup(COSINES, (phase + PATCH // 4) & (PATCH - 1))
        window_ref[rows, LANES:] = jnp.where((kz == 0) | (kz == HALF), 0.0, sine)


def prepare_kernel(index_ref, shift_ref, bank_ref, block_ref,
                   spectra_ref, window_ref, own_ref, cubes, back, sems):
    copies = [
        pltpu.make_async_copy(bank_ref.at[index_ref[0, 0, p]], cubes.at[p], sems.at[p]) for p in range(NPZ)
    ]
    for copy in copies:
        copy.start()

    window_of(shift_ref[0, 0], window_ref)
    own_ref[...] = dot3(halves(block_ref[...].reshape(HALF * HALF, LANES)), halves(window_ref[...]), 0)

    source = lax.broadcasted_iota(jnp.int32, (NPZ * PATCH, 2 * LANES), 0)
    lane = lax.broadcasted_iota(jnp.int32, (NPZ * PATCH, 2 * LANES), 1)
    p, kz = source // PATCH, source % PATCH
    target = jnp.where(kz < KZ, KZ * p + kz, LANES + KZ * p + PATCH - kz)
    pick = jnp.where(lane == target, 1.0, 0.0).astype(jnp.bfloat16)

    for copy in copies:
        copy.wait()
    total = None
    for first, last in ((0, 4), (4, NPZ)):
        joined = jnp.concatenate(
            [cubes[q].reshape(PATCH * PATCH, PATCH) for q in range(first, last)], axis=1
        )
        high, low = halves(joined)
        rows = pick[PATCH * first : PATCH * last]
        part = dot(high, rows, 0) + dot(low, rows, 0)
        total = part if total is None else total + part
    spectra_ref[...] = total[:, :LANES]
    back[...] = total[:, LANES:]
    row = lax.broadcasted_iota(jnp.int32, (SUB, LANES), 0)
    mirror = (SUB - row) % SUB
    for kx in range(PATCH):
        other = (PATCH - kx) % PATCH
        turned = [
            jnp.take_along_axis(
                back[pl.ds(other * PATCH + SUB * g, SUB), :], mirror, axis=0, mode="promise_in_bounds"
            )
            for g in range(4)
        ]
        for g in range(4):
            rows = pl.ds(kx * PATCH + SUB * g, SUB)
            mirrored = jnp.where(row == 0, turned[(4 - g) % 4], turned[3 - g])
            spectra_ref[rows, :] = spectra_ref[rows, :] + mirrored


def prepare(index, shift, bank, rhs):
    smem = pl.BlockSpec(memory_space=pltpu.SMEM)
    vmem = pl.BlockSpec(memory_space=VMEM)
    return pl.pallas_call(
        prepare_kernel,
        out_shape=[
            jax.ShapeDtypeStruct((PATCH * PATCH, LANES), jnp.float32),
            jax.ShapeDtypeStruct((LANES, 2 * LANES), jnp.float32),
            jax.ShapeDtypeStruct((HALF * HALF, 2 * LANES), jnp.float32),
        ],
        in_specs=[smem, smem, pl.BlockSpec(memory_space=pltpu.HBM), vmem],
        out_specs=[vmem] * 3,
        scratch_shapes=[
            VMEM((NPZ, PATCH, PATCH, PATCH), jnp.float32),
            VMEM((PATCH * PATCH, LANES), jnp.float32),
            pltpu.SemaphoreType.DMA((NPZ,)),
        ],
        compiler_params=pltpu.CompilerParams(vmem_limit_bytes=50 * 2**20),
        cost_estimate=pl.CostEstimate(flops=400_000_000, bytes_accessed=8_000_000, transcendentals=0),
        name="prepare",
    )(index, shift, bank, rhs)


PITCH = 40


def strided(h, y):
    return pl.ds(SUB * PITCH * h + y, SUB, stride=PITCH)


def patches_kernel(window_ref, spectra_ref, own_ref, rhs_ref, damping_ref, b10, b11, b01,
                   upper, real, imag, sums_ref, held, sums, sem):
    window = halves(window_ref[...])

    for xq, yq, block in ((0, 0, None), (1, 0, b10), (0, 1, b01), (1, 1, b11)):
        if block is None:
            result = own_ref[...]
        else:
            result = dot3(halves(block[...].reshape(HALF * HALF, LANES)), window, 0)
        for i in range(HALF):
            rows = pl.ds((HALF * xq + i) * PITCH + HALF * yq, HALF)
            real[rows, :] = result[HALF * i : HALF * (i + 1), :LANES]
            imag[rows, :] = result[HALF * i : HALF * (i + 1), LANES:]

    for h in range(4):
        out = dft32(lambda y: (real[strided(h, y), :] * TAPER[y], imag[strided(h, y), :] * TAPER[y]), -1)
        for k, (re, im) in enumerate(out):
            real[strided(h, k), :] = re
            imag[strided(h, k), :] = im

    energy = jnp.zeros((SUB, LANES), jnp.float32)
    for g in range(4):
        def rows(x):
            return pl.ds(x * PITCH + SUB * g, SUB)

        out = dft32(lambda x: (real[rows(x), :] * TAPER[x], imag[rows(x), :] * TAPER[x]), -1)
        scaled = []
        for k, (re, im) in enumerate(out):
            s = spectra_ref[pl.ds(k * PATCH + SUB * g, SUB), :]
            sre, sim = s * re, s * im
            energy = energy + (sre * re + sim * im)
            scaled.append((sre, sim))
        out = dft32(lambda k: scaled[k], 1)
        for x, (re, im) in enumerate(out):
            real[rows(x), :] = re * (TAPER[x] / PATCH**3)
            imag[rows(x), :] = im * (TAPER[x] / PATCH**3)

    square = rhs_ref[...] * rhs_ref[...]
    rr = jnp.sum(square)
    dd = jnp.sum(square * damping_ref[...]) + jnp.sum(energy) * (1.0 / PATCH**3)
    lane = lax.broadcasted_iota(jnp.int32, sums.shape, len(sums.shape) - 1)
    sums[...] = jnp.where(lane == 0, rr, jnp.where(lane == 1, dd, 0.0))
    leaving = pltpu.make_async_copy(sums, sums_ref, sem)
    leaving.start()

    for h in range(2, 4):
        out = dft32(lambda k: (real[strided(h, k), :], imag[strided(h, k), :]), 1)
        for y, (re, im) in enumerate(out):
            real[strided(h, y), :] = re * TAPER[y]
            imag[strided(h, y), :] = im * TAPER[y]
    for i in range(HALF):
        rows = pl.ds((HALF + i) * PITCH, PATCH)
        held[pl.ds(i * PATCH, PATCH), :] = jnp.concatenate([real[rows, :], imag[rows, :]], axis=1)
    upper[...] = dot3(halves(held[...]), window, 1).reshape(upper.shape)
    leaving.wait()


def patches(window, spectra, own, rhs, damping, blocks, copies):
    vmem = pl.BlockSpec(memory_space=VMEM)
    return pl.pallas_call(
        patches_kernel,
        out_shape=[jax.ShapeDtypeStruct((HALF, PATCH, LANES), jnp.float32)]
        + [jax.ShapeDtypeStruct((PATCH * PITCH, LANES), jnp.float32)] * 2
        + [jax.ShapeDtypeStruct((copies, 1, LANES), jnp.float32)],
        in_specs=[vmem] * 8,
        out_specs=[vmem] * 3 + [pl.BlockSpec(memory_space=pltpu.HBM)],
        scratch_shapes=[
            VMEM((HALF * PATCH, 2 * LANES), jnp.float32),
            VMEM((copies, 1, LANES), jnp.float32),
            pltpu.SemaphoreType.DMA,
        ],
        compiler_params=pltpu.CompilerParams(vmem_limit_bytes=32 * 2**20),
        cost_estimate=pl.CostEstimate(flops=800_000_000, bytes_accessed=4_000_000, transcendentals=0),
        name="patches",
    )(window, spectra, own, rhs, damping, *blocks)


def near_kernel(window_ref, real, imag, rhs_ref, damping_ref, arrived, image_ref, leaving_ref, held):
    for h in range(2):
        out = dft32(lambda k: (real[strided(h, k), :], imag[strided(h, k), :]), 1)
        for y, (re, im) in enumerate(out):
            held[0, strided(h, y), :] = re * TAPER[y]
            held[1, strided(h, y), :] = im * TAPER[y]
    both = [
        jnp.concatenate([held[part, pl.ds(i * PITCH, PATCH), :] for i in range(HALF)], axis=0)
        for part in range(2)
    ]
    both = jnp.concatenate(both, axis=1)
    lower = dot3(halves(both), halves(window_ref[...]), 1).reshape(arrived.shape) + arrived[...]
    image_ref[...] = lower[:, :HALF] + damping_ref[...] * rhs_ref[...]
    leaving_ref[...] = lower[:, HALF:]


def near(window, real, imag, rhs, damping, arrived):
    vmem = pl.BlockSpec(memory_space=VMEM)
    return pl.pallas_call(
        near_kernel,
        out_shape=[jax.ShapeDtypeStruct(rhs.shape, jnp.float32)] * 2,
        in_specs=[vmem] * 6,
        out_specs=[vmem] * 2,
        scratch_shapes=[VMEM((2, HALF * PITCH, LANES), jnp.float32)],
        compiler_params=pltpu.CompilerParams(vmem_limit_bytes=32 * 2**20),
        cost_estimate=pl.CostEstimate(flops=20_000_000, bytes_accessed=1_000_000, transcendentals=0),
        name="near",
    )(window, real, imag, rhs, damping, arrived)


def finish_kernel(sums_ref, rhs_ref, own, from_y, solution_ref, residual_ref, solved, left, sems):
    totals = jnp.sum(sums_ref[...], axis=(0, 1), keepdims=True)[0]
    lane = lax.broadcasted_iota(jnp.int32, totals.shape, 1)
    rr = jnp.sum(jnp.where(lane == 0, totals, 0.0), axis=1, keepdims=True)
    dd = jnp.sum(jnp.where(lane == 1, totals, 0.0), axis=1, keepdims=True)
    alpha = (rr / dd)[None]
    leaving = []
    for c in range(4):
        rows = pl.ds(4 * c, 4)
        rhs = rhs_ref[rows]
        solved[rows] = alpha * rhs
        left[rows] = rhs - alpha * (own[rows] + from_y[rows])
        for k, (source, target) in enumerate(((solved, solution_ref), (left, residual_ref))):
            copy = pltpu.make_async_copy(source.at[rows], target.at[rows], sems.at[2 * c + k])
            copy.start()
            leaving.append(copy)
    for copy in leaving:
        copy.wait()


def finish(sums, rhs, parts):
    block = jax.ShapeDtypeStruct(rhs.shape, jnp.float32)
    vmem = pl.BlockSpec(memory_space=VMEM)
    return pl.pallas_call(
        finish_kernel,
        out_shape=[block, block],
        in_specs=[vmem] * 4,
        out_specs=[pl.BlockSpec(memory_space=pltpu.HBM)] * 2,
        scratch_shapes=[VMEM(rhs.shape, jnp.float32)] * 2 + [pltpu.SemaphoreType.DMA((8,))],
        compiler_params=pltpu.CompilerParams(vmem_limit_bytes=8 * 2**20),
        cost_estimate=pl.CostEstimate(flops=1_000_000, bytes_accessed=1_000_000, transcendentals=0),
        name="finish",
    )(sums, rhs, *parts)


def moved(x, by_x, by_y):
    nx, ny = lax.axis_size("gx"), lax.axis_size("gy")
    pairs = [
        (i * ny + j, (i + by_x) * ny + j + by_y)
        for i in range(nx)
        for j in range(ny)
        if 0 <= i + by_x < nx and 0 <= j + by_y < ny
    ]
    return lax.ppermute(x, ("gx", "gy"), pairs)


def body(migrated, prior_sample, damping, psf_bank, psf_index, z_shift):
    rhs = migrated + damping * prior_sample
    nx, ny = lax.axis_size("gx"), lax.axis_size("gy")
    from_x, from_xy, from_y = moved(rhs, -1, 0), moved(rhs, -1, -1), moved(rhs, 0, -1)
    spectra, window, own = prepare(psf_index, z_shift, psf_bank, rhs)
    upper, real, imag, sums = patches(
        window, spectra, own, rhs, damping, [from_x, from_xy, from_y], nx * ny
    )
    from_x = moved(upper, 1, 0)
    sums = lax.all_to_all(sums, ("gx", "gy"), 0, 0)
    image, leaving = near(window, real, imag, rhs, damping, from_x)
    from_y = moved(leaving, 0, 1)
    return tuple(finish(sums, rhs, [image, from_y]))


def solution(mesh):
    block = P("gx", "gy", None)
    return jax.shard_map(
        body,
        mesh=mesh,
        in_specs=(block, block, block, P(), block, P("gx", "gy")),
        out_specs=(block, block),
        check_vma=False,
    )
```

```python
import math

import jax
import jax.numpy as jnp
from jax import lax
from jax.experimental import pallas as pl
from jax.experimental.pallas import tpu as pltpu
from jax.sharding import PartitionSpec as P

PATCH = 32
HALF = 16
NPZ = 6
KZ = 17
LANES = 128
SUB = 8
VMEM = pltpu.VMEM


TAPER = [math.sin(math.pi * (i + 0.5) / PATCH) for i in range(PATCH)]


def twiddle(value, k, n, sign):
    k %= n
    re, im = value
    if k == 0:
        return value
    if 4 * k == n:
        return (-im, re) if sign > 0 else (im, -re)
    if 2 * k == n:
        return (-re, -im)
    if 4 * k == 3 * n:
        return (im, -re) if sign > 0 else (-im, re)
    c = math.cos(2.0 * math.pi * k / n)
    s = sign * math.sin(2.0 * math.pi * k / n)
    if 8 * k % n == 0:
        h = abs(c)
        cs, ss = (1 if c > 0 else -1), (1 if s > 0 else -1)
        if cs == ss:
            a, b = re - im, re + im
            return (a * (h * cs), b * (h * cs))
        a, b = re + im, im - re
        return (a * (h * cs), b * (h * cs))
    return (re * c - im * s, re * s + im * c)


def add(a, b):
    return (a[0] + b[0], a[1] + b[1])


def sub(a, b):
    return (a[0] - b[0], a[1] - b[1])


def dft4(x, sign):
    a, b = add(x[0], x[2]), sub(x[0], x[2])
    c, d = add(x[1], x[3]), twiddle(sub(x[1], x[3]), 1, 4, sign)
    return [add(a, c), add(b, d), sub(a, c), sub(b, d)]


def dft8(x, sign):
    even = dft4(x[0::2], sign)
    odd = [twiddle(v, k, 8, sign) for k, v in enumerate(dft4(x[1::2], sign))]
    return [add(even[k], odd[k]) for k in range(4)] + [sub(even[k], odd[k]) for k in range(4)]


def dft32(load, sign):
    first = []
    for n2 in range(8):
        part = dft4([load(8 * n1 + n2) for n1 in range(4)], sign)
        first.append([twiddle(v, n2 * k1, 32, sign) for k1, v in enumerate(part)])
    out = [None] * 32
    for k1 in range(4):
        part = dft8([first[n2][k1] for n2 in range(8)], sign)
        for k2 in range(8):
            out[k1 + 4 * k2] = part[k2]
    return out


def halves(value):
    high = value.astype(jnp.bfloat16)
    return high, (value - high.astype(jnp.float32)).astype(jnp.bfloat16)


def dot(a, b, contract_b):
    return lax.dot_general(a, b, (((1,), (contract_b,)), ((), ())), preferred_element_type=jnp.float32)


def dot3(a, b, contract_b):
    return dot(a[0], b[0], contract_b) + (dot(a[1], b[0], contract_b) + dot(a[0], b[1], contract_b))


def lookup(values, places):
    lane = lax.broadcasted_iota(jnp.int32, (SUB, LANES), 1)
    table = jnp.zeros((SUB, LANES), jnp.float32)
    for i, value in enumerate(values):
        table = jnp.where(lane == i, value, table)
    return jnp.take_along_axis(table, places, axis=1, mode="promise_in_bounds")


COSINES = [math.cos(2.0 * math.pi * i / PATCH) for i in range(PATCH)]
COSINES[8] = COSINES[24] = 0.0


def window_of(shift, window_ref):
    lane = lax.broadcasted_iota(jnp.int32, (SUB, LANES), 1)
    p = jnp.zeros_like(lane)
    for q in range(1, NPZ):
        p = jnp.where(lane >= KZ * q, q, p)
    kz = lane - KZ * p
    first = lax.broadcasted_iota(jnp.int32, (SUB, LANES), 0) - shift - HALF * p
    for g in range(LANES // SUB):
        cell = first + SUB * g
        inside = (cell >= 0) & (cell < PATCH) & (lane < KZ * NPZ)
        cell = cell & (PATCH - 1)
        taper = jnp.where(inside, lookup(TAPER, cell), 0.0)
        phase = (kz * cell) & (PATCH - 1)
        rows = pl.ds(SUB * g, SUB)
        window_ref[rows, :LANES] = taper * lookup(COSINES, phase)
        sine = taper * lookup(COSINES, (phase + PATCH // 4) & (PATCH - 1))
        window_ref[rows, LANES:] = jnp.where((kz == 0) | (kz == HALF), 0.0, sine)


def prepare_kernel(index_ref, shift_ref, bank_ref, block_ref,
                   spectra_ref, window_ref, own_ref, cubes, back, sems):
    copies = [
        pltpu.make_async_copy(bank_ref.at[index_ref[0, 0, p]], cubes.at[p], sems.at[p]) for p in range(NPZ)
    ]
    for copy in copies:
        copy.start()

    window_of(shift_ref[0, 0], window_ref)
    own_ref[...] = dot3(halves(block_ref[...].reshape(HALF * HALF, LANES)), halves(window_ref[...]), 0)

    source = lax.broadcasted_iota(jnp.int32, (NPZ * PATCH, 2 * LANES), 0)
    lane = lax.broadcasted_iota(jnp.int32, (NPZ * PATCH, 2 * LANES), 1)
    p, kz = source // PATCH, source % PATCH
    target = jnp.where(kz < KZ, KZ * p + kz, LANES + KZ * p + PATCH - kz)
    pick = jnp.where(lane == target, 1.0, 0.0).astype(jnp.bfloat16)

    for copy in copies:
        copy.wait()
    total = None
    for first, last in ((0, 4), (4, NPZ)):
        joined = jnp.concatenate(
            [cubes[q].reshape(PATCH * PATCH, PATCH) for q in range(first, last)], axis=1
        )
        high, low = halves(joined)
        rows = pick[PATCH * first : PATCH * last]
        part = dot(high, rows, 0) + dot(low, rows, 0)
        total = part if total is None else total + part
    spectra_ref[...] = total[:, :LANES]
    back[...] = total[:, LANES:]
    row = lax.broadcasted_iota(jnp.int32, (SUB, LANES), 0)
    mirror = (SUB - row) % SUB
    for kx in range(PATCH):
        other = (PATCH - kx) % PATCH
        turned = [
            jnp.take_along_axis(
                back[pl.ds(other * PATCH + SUB * g, SUB), :], mirror, axis=0, mode="promise_in_bounds"
            )
            for g in range(4)
        ]
        for g in range(4):
            rows = pl.ds(kx * PATCH + SUB * g, SUB)
            mirrored = jnp.where(row == 0, turned[(4 - g) % 4], turned[3 - g])
            spectra_ref[rows, :] = spectra_ref[rows, :] + mirrored


def prepare(index, shift, bank, rhs):
    smem = pl.BlockSpec(memory_space=pltpu.SMEM)
    vmem = pl.BlockSpec(memory_space=VMEM)
    return pl.pallas_call(
        prepare_kernel,
        out_shape=[
            jax.ShapeDtypeStruct((PATCH * PATCH, LANES), jnp.float32),
            jax.ShapeDtypeStruct((LANES, 2 * LANES), jnp.float32),
            jax.ShapeDtypeStruct((HALF * HALF, 2 * LANES), jnp.float32),
        ],
        in_specs=[smem, smem, pl.BlockSpec(memory_space=pltpu.HBM), vmem],
        out_specs=[vmem] * 3,
        scratch_shapes=[
            VMEM((NPZ, PATCH, PATCH, PATCH), jnp.float32),
            VMEM((PATCH * PATCH, LANES), jnp.float32),
            pltpu.SemaphoreType.DMA((NPZ,)),
        ],
        compiler_params=pltpu.CompilerParams(vmem_limit_bytes=50 * 2**20),
        cost_estimate=pl.CostEstimate(flops=400_000_000, bytes_accessed=8_000_000, transcendentals=0),
        name="prepare",
    )(index, shift, bank, rhs)


PITCH = 40


def strided(h, y):
    return pl.ds(SUB * PITCH * h + y, SUB, stride=PITCH)


def patches_kernel(window_ref, spectra_ref, own_ref, rhs_ref, damping_ref, b10, b11, b01,
                   upper, real, imag, sums_ref, held, sums, sem):
    window = halves(window_ref[...])

    for xq, yq, block in ((0, 0, None), (1, 0, b10), (0, 1, b01), (1, 1, b11)):
        if block is None:
            result = own_ref[...]
        else:
            result = dot3(halves(block[...].reshape(HALF * HALF, LANES)), window, 0)
        for i in range(HALF):
            rows = pl.ds((HALF * xq + i) * PITCH + HALF * yq, HALF)
            real[rows, :] = result[HALF * i : HALF * (i + 1), :LANES]
            imag[rows, :] = result[HALF * i : HALF * (i + 1), LANES:]

    for h in range(4):
        out = dft32(lambda y: (real[strided(h, y), :] * TAPER[y], imag[strided(h, y), :] * TAPER[y]), -1)
        for k, (re, im) in enumerate(out):
            real[strided(h, k), :] = re
            imag[strided(h, k), :] = im

    energy = jnp.zeros((SUB, LANES), jnp.float32)
    for g in range(4):
        def rows(x):
            return pl.ds(x * PITCH + SUB * g, SUB)

        out = dft32(lambda x: (real[rows(x), :] * TAPER[x], imag[rows(x), :] * TAPER[x]), -1)
        scaled = []
        for k, (re, im) in enumerate(out):
            s = spectra_ref[pl.ds(k * PATCH + SUB * g, SUB), :]
            sre, sim = s * re, s * im
            energy = energy + (sre * re + sim * im)
            scaled.append((sre, sim))
        out = dft32(lambda k: scaled[k], 1)
        for x, (re, im) in enumerate(out):
            real[rows(x), :] = re * (TAPER[x] / PATCH**3)
            imag[rows(x), :] = im * (TAPER[x] / PATCH**3)

    square = rhs_ref[...] * rhs_ref[...]
    rr = jnp.sum(square)
    dd = jnp.sum(square * damping_ref[...]) + jnp.sum(energy) * (1.0 / PATCH**3)
    lane = lax.broadcasted_iota(jnp.int32, sums.shape, len(sums.shape) - 1)
    sums[...] = jnp.where(lane == 0, rr, jnp.where(lane == 1, dd, 0.0))
    leaving = pltpu.make_async_copy(sums, sums_ref, sem)
    leaving.start()

    for h in range(2, 4):
        out = dft32(lambda k: (real[strided(h, k), :], imag[strided(h, k), :]), 1)
        for y, (re, im) in enumerate(out):
            real[strided(h, y), :] = re * TAPER[y]
            imag[strided(h, y), :] = im * TAPER[y]
    for i in range(HALF):
        rows = pl.ds((HALF + i) * PITCH, PATCH)
        held[pl.ds(i * PATCH, PATCH), :] = jnp.concatenate([real[rows, :], imag[rows, :]], axis=1)
    upper[...] = dot3(halves(held[...]), window, 1).reshape(upper.shape)
    leaving.wait()


def patches(window, spectra, own, rhs, damping, blocks, copies):
    vmem = pl.BlockSpec(memory_space=VMEM)
    return pl.pallas_call(
        patches_kernel,
        out_shape=[jax.ShapeDtypeStruct((HALF, PATCH, LANES), jnp.float32)]
        + [jax.ShapeDtypeStruct((PATCH * PITCH, LANES), jnp.float32)] * 2
        + [jax.ShapeDtypeStruct((copies, 1, LANES), jnp.float32)],
        in_specs=[vmem] * 8,
        out_specs=[vmem] * 3 + [pl.BlockSpec(memory_space=pltpu.HBM)],
        scratch_shapes=[
            VMEM((HALF * PATCH, 2 * LANES), jnp.float32),
            VMEM((copies, 1, LANES), jnp.float32),
            pltpu.SemaphoreType.DMA,
        ],
        compiler_params=pltpu.CompilerParams(vmem_limit_bytes=32 * 2**20),
        cost_estimate=pl.CostEstimate(flops=800_000_000, bytes_accessed=4_000_000, transcendentals=0),
        name="patches",
    )(window, spectra, own, rhs, damping, *blocks)


def near_kernel(window_ref, real, imag, rhs_ref, damping_ref, arrived, image_ref, leaving_ref, held):
    for h in range(2):
        out = dft32(lambda k: (real[strided(h, k), :], imag[strided(h, k), :]), 1)
        for y, (re, im) in enumerate(out):
            held[0, strided(h, y), :] = re * TAPER[y]
            held[1, strided(h, y), :] = im * TAPER[y]
    both = [
        jnp.concatenate([held[part, pl.ds(i * PITCH, PATCH), :] for i in range(HALF)], axis=0)
        for part in range(2)
    ]
    both = jnp.concatenate(both, axis=1)
    lower = dot3(halves(both), halves(window_ref[...]), 1).reshape(arrived.shape) + arrived[...]
    image_ref[...] = lower[:, :HALF] + damping_ref[...] * rhs_ref[...]
    leaving_ref[...] = lower[:, HALF:]


def near(window, real, imag, rhs, damping, arrived):
    vmem = pl.BlockSpec(memory_space=VMEM)
    return pl.pallas_call(
        near_kernel,
        out_shape=[jax.ShapeDtypeStruct(rhs.shape, jnp.float32)] * 2,
        in_specs=[vmem] * 6,
        out_specs=[vmem] * 2,
        scratch_shapes=[VMEM((2, HALF * PITCH, LANES), jnp.float32)],
        compiler_params=pltpu.CompilerParams(vmem_limit_bytes=32 * 2**20),
        cost_estimate=pl.CostEstimate(flops=20_000_000, bytes_accessed=1_000_000, transcendentals=0),
        name="near",
    )(window, real, imag, rhs, damping, arrived)


def finish_kernel(sums_ref, rhs_ref, own, from_y, solution_ref, residual_ref, solved, left, sems):
    size = sums_ref.shape[0] // 8
    parts = [jnp.sum(sums_ref[pl.ds(size * c, size)], axis=0) for c in range(8)]
    while len(parts) > 1:
        parts = [a + b for a, b in zip(parts[::2], parts[1::2])]
    totals = parts[0]
    lane = lax.broadcasted_iota(jnp.int32, totals.shape, 1)
    rr = jnp.sum(jnp.where(lane == 0, totals, 0.0), axis=1, keepdims=True)
    dd = jnp.sum(jnp.where(lane == 1, totals, 0.0), axis=1, keepdims=True)
    alpha = (rr / dd)[None]
    leaving = []
    for c in range(4):
        rows = pl.ds(4 * c, 4)
        rhs = rhs_ref[rows]
        solved[rows] = alpha * rhs
        left[rows] = rhs - alpha * (own[rows] + from_y[rows])
        for k, (source, target) in enumerate(((solved, solution_ref), (left, residual_ref))):
            copy = pltpu.make_async_copy(source.at[rows], target.at[rows], sems.at[2 * c + k])
            copy.start()
            leaving.append(copy)
    for copy in leaving:
        copy.wait()


def finish(sums, rhs, parts):
    block = jax.ShapeDtypeStruct(rhs.shape, jnp.float32)
    vmem = pl.BlockSpec(memory_space=VMEM)
    return pl.pallas_call(
        finish_kernel,
        out_shape=[block, block],
        in_specs=[vmem] * 4,
        out_specs=[pl.BlockSpec(memory_space=pltpu.HBM)] * 2,
        scratch_shapes=[VMEM(rhs.shape, jnp.float32)] * 2 + [pltpu.SemaphoreType.DMA((8,))],
        compiler_params=pltpu.CompilerParams(vmem_limit_bytes=8 * 2**20),
        cost_estimate=pl.CostEstimate(flops=1_000_000, bytes_accessed=1_000_000, transcendentals=0),
        name="finish",
    )(sums, rhs, *parts)


def moved(x, by_x, by_y):
    nx, ny = lax.axis_size("gx"), lax.axis_size("gy")
    pairs = [
        (i * ny + j, (i + by_x) * ny + j + by_y)
        for i in range(nx)
        for j in range(ny)
        if 0 <= i + by_x < nx and 0 <= j + by_y < ny
    ]
    return lax.ppermute(x, ("gx", "gy"), pairs)


def body(migrated, prior_sample, damping, psf_bank, psf_index, z_shift):
    rhs = migrated + damping * prior_sample
    nx, ny = lax.axis_size("gx"), lax.axis_size("gy")
    from_x, from_xy, from_y = moved(rhs, -1, 0), moved(rhs, -1, -1), moved(rhs, 0, -1)
    spectra, window, own = prepare(psf_index, z_shift, psf_bank, rhs)
    upper, real, imag, sums = patches(
        window, spectra, own, rhs, damping, [from_x, from_xy, from_y], nx * ny
    )
    from_x = moved(upper, 1, 0)
    sums = lax.all_to_all(sums, ("gx", "gy"), 0, 0)
    image, leaving = near(window, real, imag, rhs, damping, from_x)
    from_y = moved(leaving, 0, 1)
    return tuple(finish(sums, rhs, [image, from_y]))


def solution(mesh):
    block = P("gx", "gy", None)
    return jax.shard_map(
        body,
        mesh=mesh,
        in_specs=(block, block, block, P(), block, P("gx", "gy")),
        out_specs=(block, block),
        check_vma=False,
    )
```

```python
import math

import jax
import jax.numpy as jnp
from jax import lax
from jax.experimental import pallas as pl
from jax.experimental.pallas import tpu as pltpu
from jax.sharding import PartitionSpec as P

PATCH = 32
HALF = 16
NPZ = 6
KZ = 17
LANES = 128
SUB = 8
VMEM = pltpu.VMEM


TAPER = [math.sin(math.pi * (i + 0.5) / PATCH) for i in range(PATCH)]


def twiddle(value, k, n, sign):
    k %= n
    re, im = value
    if k == 0:
        return value
    if 4 * k == n:
        return (-im, re) if sign > 0 else (im, -re)
    if 2 * k == n:
        return (-re, -im)
    if 4 * k == 3 * n:
        return (im, -re) if sign > 0 else (-im, re)
    c = math.cos(2.0 * math.pi * k / n)
    s = sign * math.sin(2.0 * math.pi * k / n)
    if 8 * k % n == 0:
        h = abs(c)
        cs, ss = (1 if c > 0 else -1), (1 if s > 0 else -1)
        if cs == ss:
            a, b = re - im, re + im
            return (a * (h * cs), b * (h * cs))
        a, b = re + im, im - re
        return (a * (h * cs), b * (h * cs))
    return (re * c - im * s, re * s + im * c)


def add(a, b):
    return (a[0] + b[0], a[1] + b[1])


def sub(a, b):
    return (a[0] - b[0], a[1] - b[1])


def dft4(x, sign):
    a, b = add(x[0], x[2]), sub(x[0], x[2])
    c, d = add(x[1], x[3]), twiddle(sub(x[1], x[3]), 1, 4, sign)
    return [add(a, c), add(b, d), sub(a, c), sub(b, d)]


def dft8(x, sign):
    even = dft4(x[0::2], sign)
    odd = [twiddle(v, k, 8, sign) for k, v in enumerate(dft4(x[1::2], sign))]
    return [add(even[k], odd[k]) for k in range(4)] + [sub(even[k], odd[k]) for k in range(4)]


def dft32(load, sign):
    first = []
    for n2 in range(8):
        part = dft4([load(8 * n1 + n2) for n1 in range(4)], sign)
        first.append([twiddle(v, n2 * k1, 32, sign) for k1, v in enumerate(part)])
    out = [None] * 32
    for k1 in range(4):
        part = dft8([first[n2][k1] for n2 in range(8)], sign)
        for k2 in range(8):
            out[k1 + 4 * k2] = part[k2]
    return out


def halves(value):
    high = value.astype(jnp.bfloat16)
    return high, (value - high.astype(jnp.float32)).astype(jnp.bfloat16)


def dot(a, b, contract_b):
    return lax.dot_general(a, b, (((1,), (contract_b,)), ((), ())), preferred_element_type=jnp.float32)


def dot3(a, b, contract_b):
    return dot(a[0], b[0], contract_b) + (dot(a[1], b[0], contract_b) + dot(a[0], b[1], contract_b))


def lookup(values, places):
    lane = lax.broadcasted_iota(jnp.int32, (SUB, LANES), 1)
    table = jnp.zeros((SUB, LANES), jnp.float32)
    for i, value in enumerate(values):
        table = jnp.where(lane == i, value, table)
    return jnp.take_along_axis(table, places, axis=1, mode="promise_in_bounds")


COSINES = [math.cos(2.0 * math.pi * i / PATCH) for i in range(PATCH)]
COSINES[8] = COSINES[24] = 0.0


def window_of(shift, window_ref):
    lane = lax.broadcasted_iota(jnp.int32, (SUB, LANES), 1)
    p = jnp.zeros_like(lane)
    for q in range(1, NPZ):
        p = jnp.where(lane >= KZ * q, q, p)
    kz = lane - KZ * p
    first = lax.broadcasted_iota(jnp.int32, (SUB, LANES), 0) - shift - HALF * p
    for g in range(LANES // SUB):
        cell = first + SUB * g
        inside = (cell >= 0) & (cell < PATCH) & (lane < KZ * NPZ)
        cell = cell & (PATCH - 1)
        taper = jnp.where(inside, lookup(TAPER, cell), 0.0)
        phase = (kz * cell) & (PATCH - 1)
        rows = pl.ds(SUB * g, SUB)
        window_ref[rows, :LANES] = taper * lookup(COSINES, phase)
        sine = taper * lookup(COSINES, (phase + PATCH // 4) & (PATCH - 1))
        window_ref[rows, LANES:] = jnp.where((kz == 0) | (kz == HALF), 0.0, sine)


def prepare_kernel(index_ref, shift_ref, bank_ref, block_ref,
                   spectra_ref, window_ref, own_ref, cubes, back, sems):
    copies = [
        pltpu.make_async_copy(bank_ref.at[index_ref[0, 0, p]], cubes.at[p], sems.at[p]) for p in range(NPZ)
    ]
    for copy in copies:
        copy.start()

    window_of(shift_ref[0, 0], window_ref)
    own_ref[...] = dot3(halves(block_ref[...].reshape(HALF * HALF, LANES)), halves(window_ref[...]), 0)

    source = lax.broadcasted_iota(jnp.int32, (NPZ * PATCH, 2 * LANES), 0)
    lane = lax.broadcasted_iota(jnp.int32, (NPZ * PATCH, 2 * LANES), 1)
    p, kz = source // PATCH, source % PATCH
    target = jnp.where(kz < KZ, KZ * p + kz, LANES + KZ * p + PATCH - kz)
    pick = jnp.where(lane == target, 1.0, 0.0).astype(jnp.bfloat16)

    for copy in copies:
        copy.wait()
    total = None
    for first, last in ((0, 4), (4, NPZ)):
        joined = jnp.concatenate(
            [cubes[q].reshape(PATCH * PATCH, PATCH) for q in range(first, last)], axis=1
        )
        high, low = halves(joined)
        rows = pick[PATCH * first : PATCH * last]
        part = dot(high, rows, 0) + dot(low, rows, 0)
        total = part if total is None else total + part
    spectra_ref[...] = total[:, :LANES]
    back[...] = total[:, LANES:]
    row = lax.broadcasted_iota(jnp.int32, (SUB, LANES), 0)
    mirror = (SUB - row) % SUB
    for kx in range(PATCH):
        other = (PATCH - kx) % PATCH
        turned = [
            jnp.take_along_axis(
                back[pl.ds(other * PATCH + SUB * g, SUB), :], mirror, axis=0, mode="promise_in_bounds"
            )
            for g in range(4)
        ]
        for g in range(4):
            rows = pl.ds(kx * PATCH + SUB * g, SUB)
            mirrored = jnp.where(row == 0, turned[(4 - g) % 4], turned[3 - g])
            spectra_ref[rows, :] = spectra_ref[rows, :] + mirrored


def prepare(index, shift, bank, rhs):
    smem = pl.BlockSpec(memory_space=pltpu.SMEM)
    vmem = pl.BlockSpec(memory_space=VMEM)
    return pl.pallas_call(
        prepare_kernel,
        out_shape=[
            jax.ShapeDtypeStruct((PATCH * PATCH, LANES), jnp.float32),
            jax.ShapeDtypeStruct((LANES, 2 * LANES), jnp.float32),
            jax.ShapeDtypeStruct((HALF * HALF, 2 * LANES), jnp.float32),
        ],
        in_specs=[smem, smem, pl.BlockSpec(memory_space=pltpu.HBM), vmem],
        out_specs=[vmem] * 3,
        scratch_shapes=[
            VMEM((NPZ, PATCH, PATCH, PATCH), jnp.float32),
            VMEM((PATCH * PATCH, LANES), jnp.float32),
            pltpu.SemaphoreType.DMA((NPZ,)),
        ],
        compiler_params=pltpu.CompilerParams(vmem_limit_bytes=50 * 2**20),
        cost_estimate=pl.CostEstimate(flops=400_000_000, bytes_accessed=8_000_000, transcendentals=0),
        name="prepare",
    )(index, shift, bank, rhs)


PITCH = 40


def strided(h, y):
    return pl.ds(SUB * PITCH * h + y, SUB, stride=PITCH)


def patches_kernel(window_ref, spectra_ref, own_ref, rhs_ref, damping_ref, b10, b11, b01,
                   upper, real, imag, sums_ref, sums, sem):
    window = halves(window_ref[...])

    for xq, yq, block in ((0, 0, None), (1, 0, b10), (0, 1, b01), (1, 1, b11)):
        if block is None:
            result = own_ref[...]
        else:
            result = dot3(halves(block[...].reshape(HALF * HALF, LANES)), window, 0)
        for i in range(HALF):
            rows = pl.ds((HALF * xq + i) * PITCH + HALF * yq, HALF)
            real[rows, :] = result[HALF * i : HALF * (i + 1), :LANES]
            imag[rows, :] = result[HALF * i : HALF * (i + 1), LANES:]

    for h in range(4):
        out = dft32(lambda y: (real[strided(h, y), :] * TAPER[y], imag[strided(h, y), :] * TAPER[y]), -1)
        for k, (re, im) in enumerate(out):
            real[strided(h, k), :] = re
            imag[strided(h, k), :] = im

    energy = jnp.zeros((SUB, LANES), jnp.float32)
    for g in range(4):
        def rows(x):
            return pl.ds(x * PITCH + SUB * g, SUB)

        out = dft32(lambda x: (real[rows(x), :] * TAPER[x], imag[rows(x), :] * TAPER[x]), -1)
        scaled = []
        for k, (re, im) in enumerate(out):
            s = spectra_ref[pl.ds(k * PATCH + SUB * g, SUB), :]
            sre, sim = s * re, s * im
            energy = energy + (sre * re + sim * im)
            scaled.append((sre, sim))
        out = dft32(lambda k: scaled[k], 1)
        for x, (re, im) in enumerate(out):
            real[rows(x), :] = re * (TAPER[x] / PATCH**3)
            imag[rows(x), :] = im * (TAPER[x] / PATCH**3)

    square = rhs_ref[...] * rhs_ref[...]
    rr = jnp.sum(square)
    dd = jnp.sum(square * damping_ref[...]) + jnp.sum(energy) * (1.0 / PATCH**3)
    lane = lax.broadcasted_iota(jnp.int32, sums.shape, len(sums.shape) - 1)
    sums[...] = jnp.where(lane == 0, rr, jnp.where(lane == 1, dd, 0.0))
    leaving = pltpu.make_async_copy(sums, sums_ref, sem)
    leaving.start()

    for h in range(2, 4):
        out = dft32(lambda k: (real[strided(h, k), :], imag[strided(h, k), :]), 1)
        for y, (re, im) in enumerate(out):
            real[strided(h, y), :] = re * TAPER[y]
            imag[strided(h, y), :] = im * TAPER[y]
    both = [
        jnp.concatenate([part[pl.ds((HALF + i) * PITCH, PATCH), :] for i in range(HALF)], axis=0)
        for part in (real, imag)
    ]
    both = jnp.concatenate(both, axis=1)
    upper[...] = dot3(halves(both), window, 1).reshape(upper.shape)
    leaving.wait()


def patches(window, spectra, own, rhs, damping, blocks, copies):
    vmem = pl.BlockSpec(memory_space=VMEM)
    return pl.pallas_call(
        patches_kernel,
        out_shape=[jax.ShapeDtypeStruct((HALF, PATCH, LANES), jnp.float32)]
        + [jax.ShapeDtypeStruct((PATCH * PITCH, LANES), jnp.float32)] * 2
        + [jax.ShapeDtypeStruct((copies, 1, LANES), jnp.float32)],
        in_specs=[vmem] * 8,
        out_specs=[vmem] * 3 + [pl.BlockSpec(memory_space=pltpu.HBM)],
        scratch_shapes=[
            VMEM((copies, 1, LANES), jnp.float32),
            pltpu.SemaphoreType.DMA,
        ],
        compiler_params=pltpu.CompilerParams(vmem_limit_bytes=32 * 2**20),
        cost_estimate=pl.CostEstimate(flops=800_000_000, bytes_accessed=4_000_000, transcendentals=0),
        name="patches",
    )(window, spectra, own, rhs, damping, *blocks)


def near_kernel(window_ref, real, imag, rhs_ref, damping_ref, arrived, image_ref, leaving_ref, held):
    for h in range(2):
        out = dft32(lambda k: (real[strided(h, k), :], imag[strided(h, k), :]), 1)
        for y, (re, im) in enumerate(out):
            held[0, strided(h, y), :] = re * TAPER[y]
            held[1, strided(h, y), :] = im * TAPER[y]
    both = [
        jnp.concatenate([held[part, pl.ds(i * PITCH, PATCH), :] for i in range(HALF)], axis=0)
        for part in range(2)
    ]
    both = jnp.concatenate(both, axis=1)
    lower = dot3(halves(both), halves(window_ref[...]), 1).reshape(arrived.shape) + arrived[...]
    image_ref[...] = lower[:, :HALF] + damping_ref[...] * rhs_ref[...]
    leaving_ref[...] = lower[:, HALF:]


def near(window, real, imag, rhs, damping, arrived):
    vmem = pl.BlockSpec(memory_space=VMEM)
    return pl.pallas_call(
        near_kernel,
        out_shape=[jax.ShapeDtypeStruct(rhs.shape, jnp.float32)] * 2,
        in_specs=[vmem] * 6,
        out_specs=[vmem] * 2,
        scratch_shapes=[VMEM((2, HALF * PITCH, LANES), jnp.float32)],
        compiler_params=pltpu.CompilerParams(vmem_limit_bytes=32 * 2**20),
        cost_estimate=pl.CostEstimate(flops=20_000_000, bytes_accessed=1_000_000, transcendentals=0),
        name="near",
    )(window, real, imag, rhs, damping, arrived)


def finish_kernel(sums_ref, rhs_ref, own, from_y, solution_ref, residual_ref, solved, left, sems):
    size = sums_ref.shape[0] // 8
    parts = [jnp.sum(sums_ref[pl.ds(size * c, size)], axis=0) for c in range(8)]
    while len(parts) > 1:
        parts = [a + b for a, b in zip(parts[::2], parts[1::2])]
    totals = parts[0]
    lane = lax.broadcasted_iota(jnp.int32, totals.shape, 1)
    rr = jnp.sum(jnp.where(lane == 0, totals, 0.0), axis=1, keepdims=True)
    dd = jnp.sum(jnp.where(lane == 1, totals, 0.0), axis=1, keepdims=True)
    alpha = (rr / dd)[None]
    leaving = []
    for c in range(4):
        rows = pl.ds(4 * c, 4)
        rhs = rhs_ref[rows]
        solved[rows] = alpha * rhs
        left[rows] = rhs - alpha * (own[rows] + from_y[rows])
        for k, (source, target) in enumerate(((solved, solution_ref), (left, residual_ref))):
            copy = pltpu.make_async_copy(source.at[rows], target.at[rows], sems.at[2 * c + k])
            copy.start()
            leaving.append(copy)
    for copy in leaving:
        copy.wait()


def finish(sums, rhs, parts):
    block = jax.ShapeDtypeStruct(rhs.shape, jnp.float32)
    vmem = pl.BlockSpec(memory_space=VMEM)
    return pl.pallas_call(
        finish_kernel,
        out_shape=[block, block],
        in_specs=[vmem] * 4,
        out_specs=[pl.BlockSpec(memory_space=pltpu.HBM)] * 2,
        scratch_shapes=[VMEM(rhs.shape, jnp.float32)] * 2 + [pltpu.SemaphoreType.DMA((8,))],
        compiler_params=pltpu.CompilerParams(vmem_limit_bytes=8 * 2**20),
        cost_estimate=pl.CostEstimate(flops=1_000_000, bytes_accessed=1_000_000, transcendentals=0),
        name="finish",
    )(sums, rhs, *parts)


def moved(x, by_x, by_y):
    nx, ny = lax.axis_size("gx"), lax.axis_size("gy")
    pairs = [
        (i * ny + j, (i + by_x) * ny + j + by_y)
        for i in range(nx)
        for j in range(ny)
        if 0 <= i + by_x < nx and 0 <= j + by_y < ny
    ]
    return lax.ppermute(x, ("gx", "gy"), pairs)


def body(migrated, prior_sample, damping, psf_bank, psf_index, z_shift):
    rhs = migrated + damping * prior_sample
    nx, ny = lax.axis_size("gx"), lax.axis_size("gy")
    from_x, from_xy, from_y = moved(rhs, -1, 0), moved(rhs, -1, -1), moved(rhs, 0, -1)
    spectra, window, own = prepare(psf_index, z_shift, psf_bank, rhs)
    upper, real, imag, sums = patches(
        window, spectra, own, rhs, damping, [from_x, from_xy, from_y], nx * ny
    )
    from_x = moved(upper, 1, 0)
    sums = lax.all_to_all(sums, ("gx", "gy"), 0, 0)
    image, leaving = near(window, real, imag, rhs, damping, from_x)
    from_y = moved(leaving, 0, 1)
    return tuple(finish(sums, rhs, [image, from_y]))


def solution(mesh):
    block = P("gx", "gy", None)
    return jax.shard_map(
        body,
        mesh=mesh,
        in_specs=(block, block, block, P(), block, P("gx", "gy")),
        out_specs=(block, block),
        check_vma=False,
    )
```
